512 devices in a mesh: pool: 32 (over z, y_hi, core), tp: 16 (over x, y_lo).
Axes of the slice: x: 4, y: 8 (y_hi: 2, y_lo: 4; y = y_hi * 4 + y_lo), z: 8, core: 2. Of those that a mesh axis runs over, the one named last changes fastest.
Arguments:
- turn_query_rows: bfloat16 [8192, 8192], P('pool', 'tp'), may hold values from -40 to 40
- turn_key_value: bfloat16 [32, 2, 256, 1024], P('pool', None, 'tp'), may hold values from -40 to 40
- prefix_page_store: bfloat16 [1024, 2, 64, 1024], P('pool', None, 'tp'), may hold values from -6 to 6
- prefix_pages: int32 [32], replicated, may hold values from 16 to 32
- holder_table: int32 [32, 32], replicated, may hold values from 0 to 31, as said below
- out_weight: bfloat16 [8192, 4096], P('tp', 'pool'), may hold values from -0.0625 to 0.0625
- row_request: int32 [256], replicated, may hold values from 0 to 31
- step_query: bfloat16 [2, 256, 8192], P(None, 'pool', 'tp'), may hold values from -40 to 40
- step_kv: bfloat16 [2, 256, 2, 1024], P(None, 'pool'), may hold values from -40 to 40
Outputs:
- prefill_out: bfloat16 [8192, 4096], P(('pool', 'tp'))
- decode_out: bfloat16 [2, 256, 8192], P(None, 'pool', 'tp')
- decode_cache: bfloat16 [32, 32, 2, 2, 64, 1024], P('pool', None, None, None, None, 'tp')
The draws below stay inside these ranges and needn't reach their ends.
Inputs may be any that keep to these rules, and one draw needn't show every extreme that they name: `holder_table`: the pages of each request form 1 aligned blocks of 32 consecutive pages; the pages of one block lie on 32 distinct holders.
All inputs are finite; a program needn't handle non-finite values.
Results may differ from the reference program's by a relative error of at most 0.024.
Values may be sent and summed in bfloat16 or wider, within the bound.
A program may use at most 128 MiB of HBM per device.

```python
import math
import jax
import jax.numpy as jnp
from jax import lax

QUERY_HEADS = 64
KEY_VALUE_HEADS = 8
HEAD_SIZE = 128
DO = 4096
PAGE_POSITIONS = 64
PREFIX_PAGE_CAP = 32
TURN_TOKENS = 256
DECODE_STEPS = 2
REQUEST_COUNT = 32
DECODE_ROWS = 256
PAGE_SLOTS = 2


def draw_turn_query_rows(key, part):
    key = jax.random.fold_in(key, 1)
    tensor_shape = (REQUEST_COUNT, TURN_TOKENS, KEY_VALUE_HEADS, QUERY_HEADS // KEY_VALUE_HEADS, HEAD_SIZE)
    sample_values = jnp.clip(jax.random.normal(key, tensor_shape, jnp.float32), -4.0, 4.0)
    return sample_values.reshape(REQUEST_COUNT * TURN_TOKENS, QUERY_HEADS * HEAD_SIZE).astype(jnp.bfloat16)


def draw_turn_key_value(key, part):
    key = jax.random.fold_in(key, 2)
    tensor_shape = (REQUEST_COUNT, 2, TURN_TOKENS, KEY_VALUE_HEADS, HEAD_SIZE)
    sample_values = jnp.clip(jax.random.normal(key, tensor_shape, jnp.float32), -4.0, 4.0)
    return sample_values.reshape(REQUEST_COUNT, 2, TURN_TOKENS, KEY_VALUE_HEADS * HEAD_SIZE).astype(jnp.bfloat16)


def draw_prefix_pages(key, part):
    key = jax.random.fold_in(key, 3)
    count_key, longest_key = jax.random.split(key)
    counts = jax.random.randint(count_key, (REQUEST_COUNT,), PREFIX_PAGE_CAP // 2, PREFIX_PAGE_CAP + 1)
    longest = jax.random.randint(longest_key, (), 0, REQUEST_COUNT)
    return counts.at[longest].set(PREFIX_PAGE_CAP).astype(jnp.int32)


def draw_holder_table(key, part):
    key = jax.random.fold_in(key, 4)
    block_keys = jax.random.split(key, PREFIX_PAGE_CAP)

    def one_order(block_key):
        return jax.random.permutation(block_key, REQUEST_COUNT)
    orders = jax.vmap(one_order)(block_keys)
    return orders.reshape(REQUEST_COUNT, PREFIX_PAGE_CAP).astype(jnp.int32)


def draw_step_query(key, part):
    key = jax.random.fold_in(key, 8)
    tensor_shape = (DECODE_STEPS, DECODE_ROWS, KEY_VALUE_HEADS, QUERY_HEADS // KEY_VALUE_HEADS, HEAD_SIZE)
    sample_values = jnp.clip(jax.random.normal(key, tensor_shape, jnp.float32), -4.0, 4.0)
    return sample_values.reshape(DECODE_STEPS, DECODE_ROWS, QUERY_HEADS * HEAD_SIZE).astype(jnp.bfloat16)


def draw_step_kv(key, part):
    key = jax.random.fold_in(key, 9)
    tensor_shape = (DECODE_STEPS, DECODE_ROWS, 2, KEY_VALUE_HEADS, HEAD_SIZE)
    sample_values = jnp.clip(jax.random.normal(key, tensor_shape, jnp.float32), -4.0, 4.0)
    return sample_values.reshape(DECODE_STEPS, DECODE_ROWS, 2, KEY_VALUE_HEADS * HEAD_SIZE).astype(jnp.bfloat16)


def set_ends(entries, own_key, least, top_value):
    extent = entries.shape
    place = [jax.random.randint(jax.random.fold_in(own_key, axis), (), 0, extent[axis]) for axis in range(len(extent))]
    entries = entries.at[tuple(place)].set(least)
    longest = extent.index(max(extent))
    place[longest] = (place[longest] + 1) % extent[longest]
    return entries.at[tuple(place)].set(top_value)


def levels(rng, extent, shards, least, top_value):
    factor_of, own = 1.0, jax.random.fold_in(rng, 6)
    for axis_at, shards_of in shards:
        heights = jnp.exp(jax.random.uniform(jax.random.fold_in(own, axis_at), (shards_of,), jnp.float32, least / len(shards), top_value / len(shards)))
        factor_of = factor_of * jnp.repeat(heights, extent[axis_at] // shards_of).reshape([-1 if axis == axis_at else 1 for axis in range(len(extent))])
    return factor_of


def gaussian(stream_key, shape, width, reach, pieces=(), kind=jnp.bfloat16):
    array = width * jax.random.normal(stream_key, shape, jnp.float32)
    if pieces:
        array = array * levels(stream_key, shape, pieces, -0.22, 0.18)
    return jnp.clip(array, -reach, reach).astype(kind)


def setup_inputs(seed: int = 0) -> dict:
    arg_keys = jax.random.split(jax.random.key(seed), 10)
    turn_query_rows = draw_turn_query_rows(jax.random.fold_in(arg_keys[9], 71), 0)
    turn_key_value = draw_turn_key_value(jax.random.fold_in(arg_keys[9], 71), 0)
    prefix_page_store = gaussian(arg_keys[2], (REQUEST_COUNT * PREFIX_PAGE_CAP, 2, PAGE_POSITIONS, KEY_VALUE_HEADS * HEAD_SIZE), 1.0, 6.0, ((0, 32), (2, 16)))
    prefix_pages = draw_prefix_pages(jax.random.fold_in(arg_keys[9], 71), 0)
    holder_table = draw_holder_table(jax.random.fold_in(arg_keys[9], 71), 0)
    out_weight = gaussian(arg_keys[5], (QUERY_HEADS * HEAD_SIZE, DO), (QUERY_HEADS * HEAD_SIZE) ** -0.5, 0.0625, ((0, 16), (1, 32)))
    row_request = set_ends(jax.random.randint(arg_keys[6], (DECODE_ROWS,), 0, REQUEST_COUNT), jax.random.fold_in(arg_keys[6], 1), 0, REQUEST_COUNT - 1).astype(jnp.int32)
    step_query = draw_step_query(jax.random.fold_in(arg_keys[9], 71), 0)
    step_kv = draw_step_kv(jax.random.fold_in(arg_keys[9], 71), 0)
    return {"turn_query_rows": turn_query_rows, "turn_key_value": turn_key_value, "prefix_page_store": prefix_page_store, "prefix_pages": prefix_pages, "holder_table": holder_table, "out_weight": out_weight, "row_request": row_request, "step_query": step_query, "step_kv": step_kv}


def gather_cache(turn_key_value, prefix_page_store, holder_table):
    pages_each_holder = PREFIX_PAGE_CAP // REQUEST_COUNT

    def per_request(request_number):
        page_index = holder_table[request_number] * PREFIX_PAGE_CAP + request_number * pages_each_holder + jnp.arange(PREFIX_PAGE_CAP, dtype=jnp.int32) // REQUEST_COUNT
        every_page = jnp.take(prefix_page_store, page_index.astype(jnp.int32), axis=0)
        every_page = jnp.transpose(every_page, (1, 0, 2, 3)).reshape(2, PREFIX_PAGE_CAP * PAGE_POSITIONS, KEY_VALUE_HEADS * HEAD_SIZE)
        return jnp.concatenate([every_page, turn_key_value[request_number]], axis=1)
    return lax.map(per_request, jnp.arange(REQUEST_COUNT, dtype=jnp.int32))

def decode_layout(cache_tensor):
    total_pages = PREFIX_PAGE_CAP + TURN_TOKENS // PAGE_POSITIONS
    page_list = jnp.transpose(cache_tensor.reshape(REQUEST_COUNT, 2, total_pages, PAGE_POSITIONS, KEY_VALUE_HEADS * HEAD_SIZE), (0, 2, 1, 3, 4))
    padding_amount = jnp.zeros((REQUEST_COUNT, PAGE_SLOTS * REQUEST_COUNT - total_pages, 2, PAGE_POSITIONS, KEY_VALUE_HEADS * HEAD_SIZE), jnp.bfloat16)
    padded = jnp.concatenate([page_list, padding_amount], axis=1)
    request_ids = jnp.arange(REQUEST_COUNT, dtype=jnp.int32)

    def per_device(device):
        page_ids = jnp.arange(PAGE_SLOTS, dtype=jnp.int32)[None, :] * REQUEST_COUNT + (device - request_ids[:, None]) % REQUEST_COUNT
        return padded[request_ids[:, None], page_ids.astype(jnp.int32)]
    return lax.map(per_device, request_ids)

def prefill(turn_query_rows, cache_tensor, prefix_pages):
    group_width = QUERY_HEADS // KEY_VALUE_HEADS
    key_total = PREFIX_PAGE_CAP * PAGE_POSITIONS + TURN_TOKENS
    position = jnp.arange(key_total, dtype=jnp.int32)
    token_index = jnp.arange(TURN_TOKENS, dtype=jnp.int32)
    score_scale = 1.0 / math.sqrt(HEAD_SIZE)

    def per_request(inputs):
        request_number, row_of_cache = inputs
        query_rows = lax.dynamic_slice_in_dim(turn_query_rows, request_number * TURN_TOKENS, TURN_TOKENS, 0).astype(jnp.float32).reshape(TURN_TOKENS, KEY_VALUE_HEADS, group_width, HEAD_SIZE)
        key_matrix = row_of_cache[0].astype(jnp.float32).reshape(key_total, KEY_VALUE_HEADS, HEAD_SIZE)
        value_matrix = row_of_cache[1].astype(jnp.float32).reshape(key_total, KEY_VALUE_HEADS, HEAD_SIZE)
        scores = jnp.einsum('qhgd,khd->hgqk', query_rows, key_matrix) * score_scale
        is_live = jnp.where(position[None, :] < PREFIX_PAGE_CAP * PAGE_POSITIONS, position[None, :] // PAGE_POSITIONS < prefix_pages[request_number], position[None, :] - PREFIX_PAGE_CAP * PAGE_POSITIONS <= token_index[:, None])
        scores = jnp.where(is_live, scores, -jnp.inf)
        top_score = lax.optimization_barrier(jnp.max(scores, axis=-1, keepdims=True))
        exponent = jnp.exp(scores - top_score)
        weights = (exponent / lax.optimization_barrier(jnp.sum(exponent, axis=-1, keepdims=True))).astype(jnp.bfloat16)
        mixture = jnp.einsum('hgqk,khd->qhgd', weights.astype(jnp.float32), value_matrix)
        return mixture.reshape(TURN_TOKENS, QUERY_HEADS * HEAD_SIZE).astype(jnp.bfloat16)
    heads_out = lax.map(per_request, (jnp.arange(REQUEST_COUNT, dtype=jnp.int32), cache_tensor))
    return heads_out.reshape(REQUEST_COUNT * TURN_TOKENS, QUERY_HEADS * HEAD_SIZE)

def decode(step_query, step_kv, cache_tensor, prefix_pages, row_request):
    group_width = QUERY_HEADS // KEY_VALUE_HEADS
    key_total = PREFIX_PAGE_CAP * PAGE_POSITIONS + TURN_TOKENS
    position = jnp.arange(key_total, dtype=jnp.int32)
    step_index = jnp.arange(DECODE_STEPS, dtype=jnp.int32)
    score_scale = 1.0 / math.sqrt(HEAD_SIZE)

    def per_row(inputs):
        request_number, query_rows, fresh_key_value = inputs
        row_of_cache = cache_tensor[request_number]
        is_live = jnp.where(position < PREFIX_PAGE_CAP * PAGE_POSITIONS, position // PAGE_POSITIONS < prefix_pages[request_number], True)
        allowed = jnp.concatenate([jnp.broadcast_to(is_live[None, :], (DECODE_STEPS, key_total)), step_index[None, :] <= step_index[:, None]], axis=1)
        key_matrix = jnp.concatenate([row_of_cache[0], fresh_key_value[:, 0]], axis=0).astype(jnp.float32).reshape(key_total + DECODE_STEPS, KEY_VALUE_HEADS, HEAD_SIZE)
        value_matrix = jnp.concatenate([row_of_cache[1], fresh_key_value[:, 1]], axis=0).astype(jnp.float32).reshape(key_total + DECODE_STEPS, KEY_VALUE_HEADS, HEAD_SIZE)
        reshaped_tensor = query_rows.astype(jnp.float32).reshape(DECODE_STEPS, KEY_VALUE_HEADS, group_width, HEAD_SIZE)
        scores = jnp.einsum('shgd,khd->shgk', reshaped_tensor, key_matrix) * score_scale
        scores = jnp.where(allowed[:, None, None, :], scores, -jnp.inf)
        top_score = lax.optimization_barrier(jnp.max(scores, axis=-1, keepdims=True))
        exponent = jnp.exp(scores - top_score)
        weights = (exponent / lax.optimization_barrier(jnp.sum(exponent, axis=-1, keepdims=True))).astype(jnp.bfloat16)
        mixture = jnp.einsum('shgk,khd->shgd', weights.astype(jnp.float32), value_matrix)
        return mixture.reshape(DECODE_STEPS, QUERY_HEADS * HEAD_SIZE).astype(jnp.bfloat16)
    rows_out = lax.map(per_row, (row_request, jnp.transpose(step_query, (1, 0, 2)), jnp.transpose(step_kv, (1, 0, 2, 3))))
    return jnp.transpose(rows_out, (1, 0, 2))

def reference(turn_query_rows, turn_key_value, prefix_page_store, prefix_pages, holder_table, out_weight, row_request, step_query, step_kv):
    cache_tensor = gather_cache(turn_key_value, prefix_page_store, holder_table)
    attention = prefill(turn_query_rows, cache_tensor, prefix_pages)
    prefill_out = jnp.dot(attention, out_weight, preferred_element_type=jnp.float32).astype(jnp.bfloat16)
    decode_out = decode(step_query, step_kv, cache_tensor, prefix_pages, row_request)
    decode_cache = decode_layout(cache_tensor)
    return (prefill_out, decode_out, decode_cache)
```

```python
import functools
import math

import jax
import jax.numpy as jnp
import numpy as np
from jax import lax
from jax.experimental import pallas as pl
from jax.experimental.pallas import tpu as pltpu
from jax.sharding import PartitionSpec as P

QUERY_HEADS = 64
KEY_VALUE_HEADS = 8
HEAD_SIZE = 128
PAGE_POSITIONS = 64
PREFIX_PAGE_CAP = 32
TURN_TOKENS = 256
DECODE_STEPS = 2
POOL = 32
TP = 16
HEADS_DEV = QUERY_HEADS // TP
SCORE_SCALE = 1.0 / math.sqrt(HEAD_SIZE)
EXP2_SCALE = SCORE_SCALE * math.log2(math.e)
DEAD = 10000.0
WEIGHT_ROWS = 512
QUERY_ROWS = 64
FRESH_ROWS = 32
BLOCK_ROWS = WEIGHT_ROWS + QUERY_ROWS + FRESH_ROWS
SLOT_ROWS = 144
KEYS = TP * SLOT_ROWS
DECODE_BLOCK = 16
VMEM_LIMIT = 56 * 1024 * 1024

MESH = pl.DeviceIdType.MESH
NT = (((1,), (1,)), ((), ()))
TN = (((0,), (0,)), ((), ()))


def remote(src, dst, send_sem, recv_sem, **axes):
    return pltpu.make_async_remote_copy(
        src_ref=src,
        dst_ref=dst,
        send_sem=send_sem,
        recv_sem=recv_sem,
        device_id=axes,
        device_id_type=MESH,
    )


def half_columns(keys, values, parity):
    low = lax.broadcasted_iota(jnp.int32, keys.shape, 1) < 64
    even = jnp.where(low, keys, pltpu.roll(values, 64, 1))
    odd = jnp.where(low, pltpu.roll(keys, 64, 1), values)
    return jnp.where(parity == 0, even, odd).astype(jnp.bfloat16)


def fetch_kernel(
    store,
    turn,
    block,
    query,
    limit,
    in_code,
    row_code,
    mixer,
    attention,
    cache_kv,
    gathered,
    pages_in,
    turn_in,
    fetched,
    by_head,
    pages_out,
    turn_out,
    page_pick,
    fetch_send,
    fetch_recv,
    head_send,
    head_recv,
    page_send,
    page_recv,
    turn_send,
    turn_recv,
    ring_send,
    ring_recv,
    pair_send,
    pair_recv,
    core_send,
    core_recv,
    own_sem,
):
    me = lax.axis_index("pool")
    rank = lax.axis_index("tp")
    z = me // 4
    y_hi = (me // 2) % 2
    core = me % 2
    other_core = me + 1 - 2 * core
    partner = me + 2 - 4 * y_hi

    barrier = pltpu.get_barrier_semaphore()

    def greet_pool(i, carry):
        pl.semaphore_signal(
            barrier, inc=1, device_id={"pool": (me + i) % POOL}, device_id_type=MESH
        )
        return carry

    def greet_tp(i, carry):
        pl.semaphore_signal(
            barrier, inc=1, device_id={"tp": (rank + i) % TP}, device_id_type=MESH
        )
        return carry

    lax.fori_loop(1, POOL, greet_pool, 0)
    lax.fori_loop(1, TP, greet_tp, 0)
    pl.semaphore_wait(barrier, POOL - 1 + TP - 1)

    def fetch_copy(i):
        to = (me + i) % POOL
        return remote(
            store.at[to], fetched.at[i], fetch_send.at[i], fetch_recv.at[i], pool=to
        )

    def start_fetch(i, carry):
        fetch_copy(i).start()
        return carry

    lax.fori_loop(1, POOL, start_fetch, 0)
    fetched[0] = store[me]

    def place(at_z, at_y):
        return ((at_z + 8) % 8) * 2 + at_y

    def ring_copy(direction, step, at_y, first=False):
        sign = 1 - 2 * direction
        at = place(z - sign * step, at_y)
        to = ((z + sign + 8) % 8) * 4 + y_hi * 2 + core
        slot = gathered.at[core, at]
        return remote(
            block if first else slot,
            slot,
            ring_send.at[direction, step, at_y],
            ring_recv.at[direction, step, at_y],
            pool=to,
        )

    def core_copy(at, first=False):
        slot = gathered.at[core, at]
        return remote(
            block if first else slot, slot, core_send.at[at], core_recv, pool=other_core
        )

    def ring_wait(direction, step, at_y):
        ring_copy(direction, step, at_y).wait_recv()

    def arrived(direction, step, at_y):
        sign = 1 - 2 * direction
        return place(z - sign * (step + 1), at_y)

    own_place = place(z, y_hi)
    pair_place = place(z, 1 - y_hi)
    pair_copy = remote(
        block, gathered.at[core, own_place], pair_send, pair_recv, pool=partner
    )
    pair_copy.start()
    for direction in range(2):
        ring_copy(direction, 0, y_hi, True).start()
    core_copy(own_place, True).start()
    own_copy = pltpu.make_async_copy(block, gathered.at[core, own_place], own_sem)
    own_copy.start()

    mix = mixer[...]

    def regroup(rows, group, kv):
        moved = jnp.dot(mix, rows, preferred_element_type=jnp.float32).astype(jnp.bfloat16)
        by_head[:, kv, pl.ds(group * 16, 16), :] = moved.reshape(KEY_VALUE_HEADS, 16, HEAD_SIZE)

    for kv in range(2):
        regroup(turn[kv], 8, kv)

    def head_copy(i, part):
        to = (rank + i) % TP
        rows = pl.ds(part * 64, 64 + 16 * part)
        return remote(
            by_head.at[to // 2, :, rows],
            cache_kv.at[rank, :, rows],
            head_send.at[part, i],
            head_recv.at[part, rank],
            tp=to,
        )

    def head_arrival(i, part):
        source = (rank + TP - i) % TP
        rows = pl.ds(part * 64, 64 + 16 * part)
        return remote(
            by_head.at[0, :, rows],
            cache_kv.at[source, :, rows],
            head_send.at[part, i],
            head_recv.at[part, source],
            tp=rank,
        )

    def forward_pair():
        pair_copy.wait_recv()
        for direction in range(2):
            ring_copy(direction, 0, 1 - y_hi).start()
        core_copy(pair_place).start()

    def ring_step(step):
        for at_y in range(2):
            for direction in range(2):
                ring_wait(direction, step - 1, at_y)
                if step < 3 or at_y == direction:
                    ring_copy(direction, step, at_y).start()
                core_copy(arrived(direction, step - 1, at_y)).start()

    for part in range(2):
        def one_group(group, carry):
            for k in range(4):
                slot = group * 4 + k

                @pl.when(slot > 0)
                def _():
                    fetch_copy(slot).wait_recv()

            rows = fetched[pl.ds(group * 4, 4)]
            for kv in range(2):
                regroup(rows[:, kv * 32 : kv * 32 + 32].reshape(128, HEAD_SIZE), group, kv)
            return carry

        lax.fori_loop(4 * part, 4 * part + 4, one_group, 0)

        def start_head(i, carry):
            head_copy(i, part).start()
            return carry

        lax.fori_loop(1, TP, start_head, 0)
        if part == 0:
            forward_pair()
    cache_kv[rank] = by_head[rank // 2]
    ring_step(1)

    def wait_heads(i, carry):
        for part in range(2):
            head_arrival(i, part).wait_recv()
        return carry

    lax.fori_loop(1, TP, wait_heads, 0)

    page_pick[...] = jnp.where(row_code[...] == in_code[...], 1.0, 0.0).astype(jnp.bfloat16)
    parity = rank % 2

    def page_group(group, carry):
        picked = []
        for kv in range(2):
            rows = cache_kv[pl.ds(group * 4, 4), kv, :128, :].reshape(512, HEAD_SIZE)
            picked.append(jnp.dot(page_pick[...], rows, preferred_element_type=jnp.float32))
        halves = half_columns(picked[0], picked[1], parity)
        pages_out[:, pl.ds(group * 16, 16), :] = halves.reshape(POOL, 16, HEAD_SIZE)
        rows = [
            cache_kv[pl.ds(group * 4, 4), kv, 128:, :].reshape(64, HEAD_SIZE).astype(jnp.float32)
            for kv in range(2)
        ]
        turn_out[group] = half_columns(rows[0], rows[1], parity)
        return carry

    lax.fori_loop(0, 4, page_group, 0)

    def page_copy(i):
        to = (me + i) % POOL
        return remote(
            pages_out.at[to], pages_in.at[i], page_send.at[i], page_recv.at[i], pool=to
        )

    def turn_copy(i):
        return remote(
            turn_out.at[i],
            turn_in.at[i],
            turn_send.at[i],
            turn_recv.at[i],
            pool=(me + i) % POOL,
        )

    def start_page(i, carry):
        page_copy(i).start()
        return carry

    lax.fori_loop(1, POOL, start_page, 0)
    for i in range(1, 4):
        turn_copy(i).start()
    pages_in[0] = pages_out[me]
    turn_in[0] = turn_out[0]

    def one_head(head):
        columns = slice(head * HEAD_SIZE, (head + 1) * HEAD_SIZE)
        keys = cache_kv[:, 0].reshape(KEYS, HEAD_SIZE)
        values = cache_kv[:, 1].reshape(KEYS, HEAD_SIZE)

        def rows_block(b, carry):
            at = pl.ds(b * 128, 128)
            scores = lax.dot_general(
                query[at, columns], keys, NT, preferred_element_type=jnp.float32
            )
            token = lax.broadcasted_iota(jnp.int32, (128, KEYS), 0) + b * 128
            scores = jnp.where(limit[...] <= token.astype(jnp.float32), scores, -jnp.inf)
            top = jnp.max(scores, axis=1, keepdims=True)
            exponent = jnp.exp2(scores * EXP2_SCALE - top * EXP2_SCALE)
            total = jnp.sum(exponent, axis=1, keepdims=True)
            mixed = jnp.dot(
                exponent.astype(jnp.bfloat16), values, preferred_element_type=jnp.float32
            )
            attention[at, columns] = (mixed / total).astype(jnp.bfloat16)
            return carry

        lax.fori_loop(0, 2, rows_block, 0)

    one_head(0)
    ring_step(2)
    one_head(1)
    ring_step(3)
    one_head(2)
    for direction in range(2):
        ring_wait(direction, 3, direction)
        core_copy(arrived(direction, 3, direction)).start()
    one_head(3)

    def finish_pool(i, carry):
        fetch_copy(i).wait_send()
        page_copy(i).wait()
        return carry

    lax.fori_loop(1, POOL, finish_pool, 0)
    for i in range(1, 4):
        turn_copy(i).wait()

    def finish_tp(i, carry):
        for part in range(2):
            head_copy(i, part).wait_send()
        return carry

    lax.fori_loop(1, TP, finish_tp, 0)
    own_copy.wait()
    pair_copy.wait_send()
    for step in range(4):
        for at_y in range(2):
            for direction in range(2):
                if step < 3 or at_y == direction:
                    ring_copy(direction, step, at_y).wait_send()

    def finish_core(i, carry):
        core_copy(i).wait_send()
        return carry

    lax.fori_loop(0, 16, finish_core, 0)
    everything = gathered.at[1 - core]
    pltpu.make_async_copy(everything, everything, core_recv).wait()


def fetch_call(*operands):
    vmem = pl.BlockSpec(memory_space=pltpu.VMEM)
    dma = pltpu.SemaphoreType.DMA
    return pl.pallas_call(
        fetch_kernel,
        out_shape=(
            jax.ShapeDtypeStruct((TURN_TOKENS, HEADS_DEV * HEAD_SIZE), jnp.bfloat16),
            jax.ShapeDtypeStruct((TP, 2, SLOT_ROWS, HEAD_SIZE), jnp.bfloat16),
            jax.ShapeDtypeStruct((2, 16, BLOCK_ROWS, HEAD_SIZE), jnp.bfloat16),
            jax.ShapeDtypeStruct((POOL, PAGE_POSITIONS, HEAD_SIZE), jnp.bfloat16),
            jax.ShapeDtypeStruct((4, PAGE_POSITIONS, HEAD_SIZE), jnp.bfloat16),
        ),
        in_specs=[vmem] * len(operands),
        out_specs=(vmem, vmem, pl.BlockSpec(memory_space=pl.ANY), vmem, vmem),
        scratch_shapes=[
            pltpu.VMEM((POOL, 64, HEAD_SIZE), jnp.bfloat16),
            pltpu.VMEM((KEY_VALUE_HEADS, 2, SLOT_ROWS, HEAD_SIZE), jnp.bfloat16),
            pltpu.VMEM((POOL, PAGE_POSITIONS, HEAD_SIZE), jnp.bfloat16),
            pltpu.VMEM((4, PAGE_POSITIONS, HEAD_SIZE), jnp.bfloat16),
            pltpu.VMEM((512, 512), jnp.bfloat16),
            dma((POOL,)),
            dma((POOL,)),
            dma((2, TP)),
            dma((2, TP)),
            dma((POOL,)),
            dma((POOL,)),
            dma((4,)),
            dma((4,)),
            dma((2, 4, 2)),
            dma((2, 4, 2)),
            dma,
            dma,
            dma((16,)),
            dma,
            dma,
        ],
        compiler_params=pltpu.CompilerParams(
            collective_id=0, has_side_effects=True, vmem_limit_bytes=VMEM_LIMIT
        ),
        name="fetch_and_prefill",
    )(*operands)


def decode_kernel(block_count, code, fresh_code, limit, cache_kv, gathered, result, rows, total, sem):
    load = pltpu.make_async_copy(
        gathered.at[:, :, pl.ds(WEIGHT_ROWS, QUERY_ROWS + FRESH_ROWS), :], rows, sem
    )
    load.start()
    total[...] = jnp.zeros_like(total)
    load.wait()
    queries = rows[:, :, :QUERY_ROWS].reshape(POOL * QUERY_ROWS, HEAD_SIZE)
    fresh = rows[:, :, QUERY_ROWS:].reshape(POOL * FRESH_ROWS, HEAD_SIZE)

    def one_block(i, carry):
        def picker(height, codes):
            at = lax.broadcasted_iota(jnp.int32, (height, 1), 0)
            wanted = (at // DECODE_BLOCK) * 256 + at % DECODE_BLOCK + i * DECODE_BLOCK
            same = codes == wanted.astype(jnp.float32)
            return jnp.where(same, 1.0, 0.0).astype(jnp.bfloat16)

        pick = picker(128, code[...])
        chosen = jnp.dot(pick, queries, preferred_element_type=jnp.float32)
        fresh_rows = jnp.dot(
            picker(64, fresh_code[...]), fresh, preferred_element_type=jnp.float32
        )
        scores = lax.dot_general(
            chosen.astype(jnp.bfloat16),
            cache_kv[:, 0].reshape(KEYS, HEAD_SIZE),
            NT,
            preferred_element_type=jnp.float32,
        )
        scores = jnp.where(limit[...] < DEAD, scores, -jnp.inf)
        top = jnp.max(scores, axis=1, keepdims=True)
        own_scores, own_values = [], []
        for step in range(DECODE_STEPS):
            keys = jnp.concatenate([fresh_rows[step * 32 : step * 32 + 16]] * 8, axis=0)
            own_values.append(
                jnp.concatenate([fresh_rows[step * 32 + 16 : step * 32 + 32]] * 8, axis=0)
            )
            score = jnp.sum(chosen * keys, axis=1, keepdims=True)
            if step == 1:
                at = lax.broadcasted_iota(jnp.int32, (128, 1), 0)
                score = jnp.where(at >= 64, score, -jnp.inf)
            own_scores.append(score)
            top = jnp.maximum(top, score)
        exponent = jnp.exp2(scores * EXP2_SCALE - top * EXP2_SCALE)
        mass = jnp.sum(exponent, axis=1, keepdims=True)
        mixed = jnp.dot(
            exponent.astype(jnp.bfloat16),
            cache_kv[:, 1].reshape(KEYS, HEAD_SIZE),
            preferred_element_type=jnp.float32,
        )
        for score, value in zip(own_scores, own_values):
            share = jnp.exp2(score * EXP2_SCALE - top * EXP2_SCALE)
            mass = mass + share
            mixed = mixed + share * value
        out = (mixed / mass).astype(jnp.bfloat16)
        total[...] += lax.dot_general(pick, out, TN, preferred_element_type=jnp.float32)
        return carry

    lax.fori_loop(0, block_count[0], one_block, 0)
    result[...] = total[...].astype(jnp.bfloat16)


def decode_call(*operands):
    vmem = pl.BlockSpec(memory_space=pltpu.VMEM)
    return pl.pallas_call(
        decode_kernel,
        out_shape=jax.ShapeDtypeStruct((POOL * QUERY_ROWS, HEAD_SIZE), jnp.bfloat16),
        in_specs=[pl.BlockSpec(memory_space=pltpu.SMEM)]
        + [vmem] * 4
        + [pl.BlockSpec(memory_space=pl.ANY)],
        out_specs=vmem,
        scratch_shapes=[
            pltpu.VMEM((2, 16, QUERY_ROWS + FRESH_ROWS, HEAD_SIZE), jnp.bfloat16),
            pltpu.VMEM((POOL * QUERY_ROWS, HEAD_SIZE), jnp.float32),
            pltpu.SemaphoreType.DMA,
        ],
        compiler_params=pltpu.CompilerParams(vmem_limit_bytes=VMEM_LIMIT),
        name="decode_rows",
    )(*operands)


CHUNKS = 4
CHUNK = 1024


def project_kernel(
    attention,
    decoded,
    gathered,
    out,
    decode_out,
    weight,
    partial,
    from_x,
    mid,
    from_y,
    from_pool,
    weight_sem,
    pool_send,
    pool_recv,
    x_send,
    x_recv,
    y_send,
    y_recv,
):
    me = lax.axis_index("pool")
    rank = lax.axis_index("tp")
    x = rank // 4
    y = rank % 4

    def weight_copy(chunk):
        places = pl.ds(chunk * 4, 4)
        return pltpu.make_async_copy(
            gathered.at[:, places, pl.ds(0, WEIGHT_ROWS), :],
            weight.at[:, places],
            weight_sem.at[chunk],
        )

    for chunk in range(CHUNKS):
        weight_copy(chunk).start()

    barrier = pltpu.get_barrier_semaphore()

    def greet_pool(i, carry):
        pl.semaphore_signal(
            barrier, inc=1, device_id={"pool": (me + i) % POOL}, device_id_type=MESH
        )
        return carry

    lax.fori_loop(1, POOL, greet_pool, 0)
    for i in range(1, 4):
        pl.semaphore_signal(
            barrier, inc=1, device_id={"tp": ((x + i) % 4) * 4 + y}, device_id_type=MESH
        )
        pl.semaphore_signal(
            barrier, inc=1, device_id={"tp": x * 4 + (y + i) % 4}, device_id_type=MESH
        )
    pl.semaphore_wait(barrier, POOL - 1 + 6)

    def pool_copy(i):
        to = (me + i) % POOL
        return remote(
            decoded.at[(to % 2) * 16 + to // 2],
            from_pool.at[i],
            pool_send.at[i],
            pool_recv.at[i],
            pool=to,
        )

    def x_copy(chunk, i):
        to = (x + i) % 4
        return remote(
            partial.at[chunk, pl.ds(to * 64, 64)],
            from_x.at[chunk, i],
            x_send.at[chunk, i],
            x_recv.at[chunk, i],
            tp=to * 4 + y,
        )

    def y_copy(chunk, i):
        to = (y + i) % 4
        return remote(
            mid.at[chunk, pl.ds(to * 16, 16)],
            from_y.at[chunk, i],
            y_send.at[chunk, i],
            y_recv.at[chunk, i],
            tp=x * 4 + to,
        )

    for chunk in range(CHUNKS):
        weight_copy(chunk).wait()

        def one_place(i, carry):
            for core in range(2):
                product = jnp.dot(
                    attention[...],
                    weight[core, chunk * 4 + i],
                    preferred_element_type=jnp.float32,
                )
                columns = pl.ds(pl.multiple_of(i * 256 + core * 128, 128), 128)
                partial[chunk, :, columns] = product.astype(jnp.bfloat16)
            return carry

        lax.fori_loop(0, 4, one_place, 0)
        for i in (2, 1, 3):
            x_copy(chunk, i).start()

    def start_pool(i, carry):
        pool_copy(i).start()
        return carry

    lax.fori_loop(1, POOL, start_pool, 0)
    from_pool[0] = decoded[(me % 2) * 16 + me // 2]

    for chunk in range(CHUNKS):
        for i in range(1, 4):
            x_copy(chunk, i).wait_recv()
        rows = partial[chunk, pl.ds(x * 64, 64), :].astype(jnp.float32)
        for i in range(1, 4):
            rows = rows + from_x[chunk, i].astype(jnp.float32)
        mid[chunk] = rows.astype(jnp.bfloat16)
        for i in range(1, 4):
            y_copy(chunk, i).start()

    def wait_pool(i, carry):
        pool_copy(i).wait()
        return carry

    lax.fori_loop(1, POOL, wait_pool, 0)

    def add_pool(i, carry):
        return carry + from_pool[i].astype(jnp.float32)

    decode_out[...] = lax.fori_loop(
        0, POOL, add_pool, jnp.zeros((QUERY_ROWS, HEAD_SIZE), jnp.float32)
    ).astype(jnp.bfloat16)

    for chunk in range(CHUNKS):
        for i in range(1, 4):
            y_copy(chunk, i).wait_recv()
        rows = mid[chunk, pl.ds(y * 16, 16), :].astype(jnp.float32)
        for i in range(1, 4):
            rows = rows + from_y[chunk, i].astype(jnp.float32)
        out[:, chunk * CHUNK : (chunk + 1) * CHUNK] = rows.astype(jnp.bfloat16)
    for chunk in range(CHUNKS):
        for i in range(1, 4):
            x_copy(chunk, i).wait_send()
            y_copy(chunk, i).wait_send()


def project_call(attention, decoded, gathered):
    vmem = pl.BlockSpec(memory_space=pltpu.VMEM)
    dma = pltpu.SemaphoreType.DMA
    return pl.pallas_call(
        project_kernel,
        out_shape=(
            jax.ShapeDtypeStruct((16, CHUNKS * CHUNK), jnp.bfloat16),
            jax.ShapeDtypeStruct((QUERY_ROWS, HEAD_SIZE), jnp.bfloat16),
        ),
        in_specs=[vmem, vmem, pl.BlockSpec(memory_space=pl.ANY)],
        out_specs=(vmem, vmem),
        scratch_shapes=[
            pltpu.VMEM((2, 16, WEIGHT_ROWS, HEAD_SIZE), jnp.bfloat16),
            pltpu.VMEM((CHUNKS, TURN_TOKENS, CHUNK), jnp.bfloat16),
            pltpu.VMEM((CHUNKS, 4, 64, CHUNK), jnp.bfloat16),
            pltpu.VMEM((CHUNKS, 64, CHUNK), jnp.bfloat16),
            pltpu.VMEM((CHUNKS, 4, 16, CHUNK), jnp.bfloat16),
            pltpu.VMEM((POOL, QUERY_ROWS, HEAD_SIZE), jnp.bfloat16),
            dma((CHUNKS,)),
            dma((POOL,)),
            dma((POOL,)),
            dma((CHUNKS, 4)),
            dma((CHUNKS, 4)),
            dma((CHUNKS, 4)),
            dma((CHUNKS, 4)),
        ],
        compiler_params=pltpu.CompilerParams(
            collective_id=1, has_side_effects=True, vmem_limit_bytes=VMEM_LIMIT
        ),
        name="project_and_return",
    )(attention, decoded, gathered)


def mixing_matrix():
    matrix = np.zeros((128, 128), np.float32)
    for head in range(8):
        for position in range(16):
            matrix[head * 16 + position, position * 8 + head] = 1
    return matrix


def page_codes():
    at = np.arange(512)
    return (((at % 128) // 4) * 16 + (at // 128) * 4 + at % 4).astype(np.float32)[None]


def per_device(
    turn_query_rows,
    turn_key_value,
    prefix_page_store,
    prefix_pages,
    holder_table,
    out_weight,
    row_request,
    step_query,
    step_kv,
):
    me = lax.axis_index("pool")
    rank = lax.axis_index("tp")
    store = prefix_page_store.reshape(POOL, 64, HEAD_SIZE)
    turn = turn_key_value.reshape(2, 128, HEAD_SIZE)
    queries = jnp.transpose(
        step_query.reshape(DECODE_STEPS, 8, HEADS_DEV, HEAD_SIZE), (0, 2, 1, 3)
    ).reshape(QUERY_ROWS, HEAD_SIZE)
    fresh = lax.dynamic_slice_in_dim(step_kv, (rank // 2) * HEAD_SIZE, HEAD_SIZE, 3)
    fresh = jnp.transpose(fresh, (0, 2, 1, 3)).reshape(FRESH_ROWS, HEAD_SIZE)
    block = jnp.concatenate([out_weight, queries, fresh], axis=0)

    holders = lax.dynamic_index_in_dim(holder_table, me, 0, keepdims=False)
    slot_of_page = (me - holders) % POOL
    live_pages = lax.dynamic_index_in_dim(prefix_pages, me, 0, keepdims=False)
    pages = jnp.arange(PREFIX_PAGE_CAP, dtype=jnp.int32)
    is_slot = slot_of_page[None, :] == pages[:, None]
    slot_live = jnp.any(is_slot & (pages[None, :] < live_pages), axis=1)
    slot_limit = jnp.where(slot_live, -1.0, DEAD)
    row = jnp.arange(SLOT_ROWS, dtype=jnp.int32)
    turn_position = jnp.arange(TP, dtype=jnp.float32)[:, None] * 16 + (row - 128)[None, :]
    limit = jnp.where(
        row[None, :] < 128, jnp.pad(jnp.repeat(slot_limit, 4), (0, 16))[None, :], turn_position
    ).reshape(1, KEYS)
    slot_for_target = jnp.roll(slot_of_page, me)
    row_code = (slot_for_target[:, None] * 16 + jnp.arange(16, dtype=jnp.int32)[None, :]).reshape(
        512, 1
    )

    attention, cache_kv, gathered, pages_in, turn_in = fetch_call(
        store,
        turn,
        block,
        turn_query_rows,
        limit,
        jnp.asarray(page_codes()),
        row_code.astype(jnp.float32),
        jnp.asarray(mixing_matrix(), jnp.bfloat16),
    )

    match = row_request == me
    row_ids = jnp.arange(256, dtype=jnp.int32)
    before = jnp.sum(
        jnp.where((row_ids[None, :] < row_ids[:, None]) & match[None, :], 1, 0), axis=1
    )
    block_count = (jnp.sum(match.astype(jnp.int32)) + DECODE_BLOCK - 1) // DECODE_BLOCK
    order = jnp.where(match, before, -10000).reshape(16, 2, 8)
    order = jnp.transpose(order, (1, 0, 2)).reshape(POOL, 1, 8)
    code = order + 256 * jnp.arange(8, dtype=jnp.int32)[None, :, None]
    fresh_code = order + 256 * jnp.arange(4, dtype=jnp.int32)[None, :, None]
    decoded = decode_call(
        block_count.reshape(1),
        code.reshape(1, POOL * QUERY_ROWS).astype(jnp.float32),
        fresh_code.reshape(1, POOL * FRESH_ROWS).astype(jnp.float32),
        limit,
        cache_kv,
        gathered,
    )
    prefill_out, decode_rows = project_call(
        attention, decoded.reshape(POOL, QUERY_ROWS, HEAD_SIZE), gathered
    )
    decode_out = jnp.transpose(
        decode_rows.reshape(DECODE_STEPS, HEADS_DEV, 8, HEAD_SIZE), (0, 2, 1, 3)
    ).reshape(DECODE_STEPS, 8, HEADS_DEV * HEAD_SIZE)

    slot = (me - pages) % POOL
    prefix_part = jnp.take(pages_in, slot, axis=0)
    turn_part = jnp.where(
        (slot < 4)[:, None, None], jnp.take(turn_in, jnp.minimum(slot, 3), axis=0), 0
    )
    both = jnp.stack([prefix_part, turn_part], axis=1)
    decode_cache = jnp.stack([both[..., :64], both[..., 64:]], axis=2)[None]
    return (prefill_out, decode_out, decode_cache)


def solution(mesh):
    placed = (
        P("pool", "tp"),
        P("pool", None, "tp", None),
        P("pool", None, "tp", None),
        P(),
        P(),
        P("tp", "pool"),
        P(),
        P(None, "pool", "tp"),
        P(None, "pool", None, None),
    )
    return jax.shard_map(
        per_device,
        mesh=mesh,
        in_specs=placed,
        out_specs=(
            P(("pool", "tp"), None),
            P(None, "pool", "tp"),
            P("pool", None, None, None, None, "tp"),
        ),
        check_vma=False,
    )
```

```python
import math

import jax
import jax.numpy as jnp
from jax import lax
from jax.experimental import pallas as pl
from jax.experimental.pallas import tpu as pltpu
from jax.sharding import PartitionSpec as P

QUERY_HEADS = 64
KEY_VALUE_HEADS = 8
HEAD_SIZE = 128
PAGE_POSITIONS = 64
PREFIX_PAGE_CAP = 32
TURN_TOKENS = 256
DECODE_STEPS = 2
POOL = 32
TP = 16
HEADS_DEV = QUERY_HEADS // TP
SCORE_SCALE = 1.0 / math.sqrt(HEAD_SIZE)
EXP2_SCALE = SCORE_SCALE * math.log2(math.e)
WEIGHT_ROWS = 512
QUERY_ROWS = 64
FRESH_ROWS = 32
BLOCK_ROWS = WEIGHT_ROWS + QUERY_ROWS + FRESH_ROWS
TURN_ROWS = TURN_TOKENS // TP
KEYS = PREFIX_PAGE_CAP * PAGE_POSITIONS
CHUNKS = 4
CHUNK = 1024
VMEM_LIMIT = 56 * 1024 * 1024

MESH = pl.DeviceIdType.MESH
NT = (((1,), (1,)), ((), ()))


def remote(src, dst, send_sem, recv_sem, **axes):
    return pltpu.make_async_remote_copy(
        src_ref=src,
        dst_ref=dst,
        send_sem=send_sem,
        recv_sem=recv_sem,
        device_id=axes,
        device_id_type=MESH,
    )


def wait_bytes(like, sem):
    pltpu.make_async_copy(like, like, sem).wait()


def half_columns(keys, values, parity):
    low = lax.broadcasted_iota(jnp.int32, keys.shape, 1) < 64
    even = jnp.where(low, keys, pltpu.roll(values, 64, 1))
    odd = jnp.where(low, pltpu.roll(keys, 64, 1), values)
    return jnp.where(parity == 0, even, odd).astype(jnp.bfloat16)


def iota(shape, dimension):
    return lax.broadcasted_iota(jnp.int32, shape, dimension)


def one_hot(condition):
    return jnp.where(condition, 1.0, 0.0).astype(jnp.bfloat16)


def layer_kernel(
    prefix_pages,
    holder_table,
    row_group,
    store,
    turn,
    weight,
    rows_to_ring,
    query,
    out,
    decode_out,
    pages_in,
    turn_in,
    gathered,
    fetched,
    by_head,
    turn_by_head,
    cache_kv,
    turn_kv,
    pages_out,
    turn_out,
    page_pick,
    live_bias,
    attention,
    decoded,
    from_pool,
    partial,
    from_x,
    mid,
    from_y,
    fetch_send,
    fetch_recv,
    head_send,
    head_recv,
    turn_head_send,
    turn_head_recv,
    page_send,
    page_recv,
    turn_send,
    turn_recv,
    ring_send,
    ring_recv,
    pair_send,
    pair_recv,
    core_send,
    core_recv,
    own_sem,
    pool_send,
    pool_recv,
    x_send,
    x_recv,
    y_send,
    y_recv,
):
    me = lax.axis_index("pool")
    rank = lax.axis_index("tp")
    z = me // 4
    y_hi = (me // 2) % 2
    core = me % 2
    x = rank // 4
    y = rank % 4
    other_core = me + 1 - 2 * core
    partner = me + 2 - 4 * y_hi

    barrier = pltpu.get_barrier_semaphore()

    def greet_pool(i, carry):
        pl.semaphore_signal(
            barrier, inc=1, device_id={"pool": (me + i) % POOL}, device_id_type=MESH
        )
        return carry

    def greet_tp(i, carry):
        pl.semaphore_signal(
            barrier, inc=1, device_id={"tp": (rank + i) % TP}, device_id_type=MESH
        )
        return carry

    lax.fori_loop(1, POOL, greet_pool, 0)
    lax.fori_loop(1, TP, greet_tp, 0)

    def place(at_z, at_y):
        return ((at_z + 8) % 8) * 2 + at_y

    own_place = place(z, y_hi)
    pair_place = place(z, 1 - y_hi)
    own_block = gathered.at[core, own_place]
    weight_copy = pltpu.make_async_copy(
        weight, own_block.at[pl.ds(0, WEIGHT_ROWS)], own_sem.at[0]
    )
    rows_copy = pltpu.make_async_copy(
        rows_to_ring, own_block.at[pl.ds(WEIGHT_ROWS, QUERY_ROWS + FRESH_ROWS)], own_sem.at[1]
    )
    weight_copy.start()
    rows_copy.start()

    slots = (me + POOL - holder_table[pl.ds(me, 1), :]) % POOL
    square = (POOL, PREFIX_PAGE_CAP)
    slot_column = jnp.sum(
        jnp.where(iota(square, 0) == iota(square, 1), slots, 0), axis=1, keepdims=True
    )
    wide = (PREFIX_PAGE_CAP, 128)
    slot_live = jnp.max(
        jnp.where(
            (slot_column == iota(wide, 1) // 4) & (iota(wide, 0) < prefix_pages[me]), 1.0, 0.0
        ),
        axis=0,
        keepdims=True,
    )
    bias = jnp.where(slot_live > 0.0, 0.0, -jnp.inf)
    live_bias[...] = jnp.concatenate([bias] * TP, axis=1)
    tall = (512, PREFIX_PAGE_CAP)
    wanted_page = (iota(tall, 0) // 16 + POOL - me) % POOL
    row_slot = jnp.sum(
        jnp.where(iota(tall, 1) == wanted_page, slots, 0), axis=1, keepdims=True
    )
    row_code = row_slot * 16 + iota((512, 1), 0) % 16
    lane = iota((1, 512), 1)
    lane_code = ((lane % 128) // 4) * 16 + (lane // 128) * 4 + lane % 4
    page_pick[...] = one_hot(row_code == lane_code)
    mix_at = iota((128, 128), 0)
    mix = one_hot((mix_at % 16) * 8 + mix_at // 16 == iota((128, 128), 1))
    for kv in range(2):
        for head in range(KEY_VALUE_HEADS):
            turn_by_head[head, kv] = turn[kv, :, head * HEAD_SIZE : (head + 1) * HEAD_SIZE]
    weight_copy.wait()
    rows_copy.wait()

    pl.semaphore_wait(barrier, POOL - 1 + TP - 1)

    def fetch_copy(i):
        to = (me + i) % POOL
        return remote(
            store.at[to], fetched.at[i], fetch_send, fetch_recv.at[i // 4], pool=to
        )

    def start_fetch(i, carry):
        fetch_copy(i).start()
        return carry

    lax.fori_loop(1, POOL, start_fetch, 0)

    def ring_copy(direction, step, at_y):
        sign = 1 - 2 * direction
        slot = gathered.at[core, place(z - sign * step, at_y)]
        to = ((z + sign + 8) % 8) * 4 + y_hi * 2 + core
        return remote(slot, slot, ring_send, ring_recv.at[direction, step, at_y], pool=to)

    def core_copy(at):
        slot = gathered.at[core, at]
        return remote(slot, slot, core_send, core_recv, pool=other_core)

    def arrived(direction, step, at_y):
        sign = 1 - 2 * direction
        return place(z - sign * (step + 1), at_y)

    pair_copy = remote(own_block, own_block, pair_send, pair_recv, pool=partner)
    pair_copy.start()
    for direction in range(2):
        ring_copy(direction, 0, y_hi).start()

    def turn_head_copy(i):
        to = (rank + i) % TP
        return remote(
            turn_by_head.at[to // 2], turn_kv.at[rank], turn_head_send, turn_head_recv, tp=to
        )

    def start_turn_head(i, carry):
        turn_head_copy(i).start()
        return carry

    lax.fori_loop(1, TP, start_turn_head, 0)
    core_copy(own_place).start()
    fetched[0] = store[me]
    turn_kv[rank] = turn_by_head[rank // 2]

    def head_copy(i, part):
        to = (rank + i) % TP
        rows = pl.ds(part * 64, 64)
        return remote(
            by_head.at[to // 2, :, rows], cache_kv.at[rank, :, rows], head_send, head_recv, tp=to
        )

    def forward_pair():
        pair_copy.wait_recv()
        for direction in range(2):
            ring_copy(direction, 0, 1 - y_hi).start()
        core_copy(pair_place).start()

    def ring_step(step):
        for at_y in range(2):
            for direction in range(2):
                ring_copy(direction, step - 1, at_y).wait_recv()
                if step < 3 or at_y == direction:
                    ring_copy(direction, step, at_y).start()
                core_copy(arrived(direction, step - 1, at_y)).start()

    for part in range(2):

        def one_group(group, carry):
            rows = fetched[pl.ds(group * 4, 4)]
            for kv in range(2):
                moved = jnp.dot(
                    mix,
                    rows[:, kv * 32 : kv * 32 + 32].reshape(128, HEAD_SIZE),
                    preferred_element_type=jnp.float32,
                ).astype(jnp.bfloat16)
                by_head[:, kv, pl.ds(group * 16, 16), :] = moved.reshape(
                    KEY_VALUE_HEADS, 16, HEAD_SIZE
                )
            return carry

        def wait_group(group, carry):
            wait_bytes(fetched.at[pl.ds(group * 4, 4)], fetch_recv.at[group])
            return one_group(group, carry)

        if part == 0:
            wait_bytes(fetched.at[pl.ds(1, 3)], fetch_recv.at[0])
            one_group(0, 0)
            lax.fori_loop(1, 4, wait_group, 0)
        else:
            lax.fori_loop(4, 8, wait_group, 0)

        def start_head(i, carry):
            head_copy(i, part).start()
            return carry

        lax.fori_loop(1, TP, start_head, 0)
        if part == 0:
            forward_pair()
    cache_kv[rank] = by_head[rank // 2]
    ring_step(1)
    ring_step(2)
    wait_bytes(cache_kv.at[pl.ds(0, TP - 1)], head_recv)
    wait_bytes(turn_kv.at[pl.ds(0, TP - 1)], turn_head_recv)

    parity = rank % 2

    def page_group(group, carry):
        members = pl.ds(group * 4, 4)
        rows = [
            cache_kv[members, kv].reshape(512, HEAD_SIZE).astype(jnp.float32) for kv in range(2)
        ]
        halves = half_columns(rows[0], rows[1], parity)
        picked = jnp.dot(page_pick[...], halves, preferred_element_type=jnp.float32)
        pages_out[:, pl.ds(group * 16, 16), :] = picked.astype(jnp.bfloat16).reshape(
            POOL, 16, HEAD_SIZE
        )
        rows = [
            turn_kv[members, kv].reshape(64, HEAD_SIZE).astype(jnp.float32) for kv in range(2)
        ]
        turn_out[group] = half_columns(rows[0], rows[1], parity)
        return carry

    lax.fori_loop(0, 4, page_group, 0)

    def start_page(i, carry):
        to = (me + i) % POOL
        remote(pages_out.at[to], pages_in.at[i], page_send, page_recv, pool=to).start()
        return carry

    def start_turn(i, carry):
        remote(
            turn_out.at[i], turn_in.at[i], turn_send, turn_recv, pool=(me + i) % POOL
        ).start()
        return carry

    lax.fori_loop(1, POOL, start_page, 0)
    lax.fori_loop(1, 4, start_turn, 0)
    pages_in[0] = pages_out[me]
    turn_in[0] = turn_out[0]

    def attend(rows, prefix_bias, turn_mask, fresh):
        scores = lax.dot_general(
            rows,
            cache_kv[:, 0].reshape(KEYS, HEAD_SIZE),
            NT,
            preferred_element_type=jnp.float32,
        )
        scores = scores + prefix_bias
        turn_scores = lax.dot_general(
            rows,
            turn_kv[:, 0].reshape(TURN_TOKENS, HEAD_SIZE),
            NT,
            preferred_element_type=jnp.float32,
        )
        if turn_mask is not None:
            turn_scores = jnp.where(turn_mask, turn_scores, -jnp.inf)
        top = jnp.maximum(
            jnp.max(scores, axis=1, keepdims=True), jnp.max(turn_scores, axis=1, keepdims=True)
        )
        for score, _ in fresh:
            top = jnp.maximum(top, score)
        top = top * EXP2_SCALE
        exponent = jnp.exp2(scores * EXP2_SCALE - top)
        turn_exponent = jnp.exp2(turn_scores * EXP2_SCALE - top)
        total = jnp.sum(exponent, axis=1, keepdims=True) + jnp.sum(
            turn_exponent, axis=1, keepdims=True
        )
        mixed = jnp.dot(
            exponent.astype(jnp.bfloat16),
            cache_kv[:, 1].reshape(KEYS, HEAD_SIZE),
            preferred_element_type=jnp.float32,
        ) + jnp.dot(
            turn_exponent.astype(jnp.bfloat16),
            turn_kv[:, 1].reshape(TURN_TOKENS, HEAD_SIZE),
            preferred_element_type=jnp.float32,
        )
        for score, value in fresh:
            share = jnp.exp2(score * EXP2_SCALE - top)
            total = total + share
            mixed = mixed + share * value
        return (mixed / total).astype(jnp.bfloat16)

    def one_head(head):
        columns = slice(head * HEAD_SIZE, (head + 1) * HEAD_SIZE)

        def rows_block(b, carry):
            at = pl.ds(b * 128, 128)
            causal = (128, TURN_TOKENS)
            mask = iota(causal, 1) <= iota(causal, 0) + b * 128
            attention[at, columns] = attend(query[at, columns], live_bias[...], mask, ())
            return carry

        lax.fori_loop(0, 2, rows_block, 0)

    one_head(0)
    ring_step(3)
    one_head(1)
    one_head(2)
    for direction in range(2):
        ring_copy(direction, 3, direction).wait_recv()
        core_copy(arrived(direction, 3, direction)).start()
    one_head(3)
    wait_bytes(gathered.at[1 - core], core_recv)

    def x_copy(chunk, i):
        to = (x + i) % 4
        return remote(
            partial.at[chunk, pl.ds(to * 64, 64)],
            from_x.at[chunk, i],
            x_send,
            x_recv.at[chunk],
            tp=to * 4 + y,
        )

    def y_copy(chunk, i):
        to = (y + i) % 4
        return remote(
            mid.at[chunk, pl.ds(to * 16, 16)],
            from_y.at[chunk, i],
            y_send,
            y_recv.at[chunk],
            tp=x * 4 + to,
        )

    def project(chunk, carry):
        def one_place(i, inner):
            for part_core in range(2):
                product = jnp.dot(
                    attention[...],
                    gathered[part_core, chunk * 4 + i, :WEIGHT_ROWS],
                    preferred_element_type=jnp.float32,
                )
                columns = pl.ds(pl.multiple_of(i * 256 + part_core * 128, 128), 128)
                partial[chunk, :, columns] = product.astype(jnp.bfloat16)
            return inner

        lax.fori_loop(0, 4, one_place, 0)
        for i in (2, 1, 3):
            x_copy(chunk, i).start()
        return carry

    lax.fori_loop(0, CHUNKS, project, 0)

    def decode_block(b, carry):
        part_core = b // 8
        places = pl.ds((b % 8) * 2, 2)
        rows = gathered[part_core, places, WEIGHT_ROWS : WEIGHT_ROWS + QUERY_ROWS].reshape(
            128, HEAD_SIZE
        )
        fresh_rows = (
            gathered[part_core, places, WEIGHT_ROWS + QUERY_ROWS :]
            .astype(jnp.float32)
            .reshape(2, 4, 1, 8, HEAD_SIZE)
        )
        rows_wide = rows.astype(jnp.float32)
        fresh = []
        for step in range(DECODE_STEPS):
            key, value = (
                jnp.broadcast_to(fresh_rows[:, 2 * step + kv], (2, 8, 8, HEAD_SIZE)).reshape(
                    128, HEAD_SIZE
                )
                for kv in range(2)
            )
            score = jnp.sum(rows_wide * key, axis=1, keepdims=True)
            if step == 1:
                score = jnp.where(iota((128, 1), 0) % 64 >= 32, score, -jnp.inf)
            fresh.append((score, value))
        result = attend(rows, live_bias[...], None, fresh).reshape(2, QUERY_ROWS, HEAD_SIZE)
        for k in range(2):
            to = ((b % 8) * 2 + k) * 2 + part_core
            slot = (to - me + POOL) % POOL
            decoded[slot] = result[k]

            @pl.when(slot > 0)
            def _():
                remote(
                    decoded.at[slot], from_pool.at[slot], pool_send, pool_recv, pool=to
                ).start()

        return carry

    def add_x(chunk):
        wait_bytes(from_x.at[chunk, pl.ds(1, 3)], x_recv.at[chunk])
        rows = partial[chunk, pl.ds(x * 64, 64), :].astype(jnp.float32)
        for i in range(1, 4):
            rows = rows + from_x[chunk, i].astype(jnp.float32)
        mid[chunk] = rows.astype(jnp.bfloat16)
        for i in range(1, 4):
            y_copy(chunk, i).start()

    def decode_and_add(chunk, carry):
        lax.fori_loop(4 * chunk, 4 * chunk + 4, decode_block, 0)
        add_x(chunk)
        return carry

    lax.fori_loop(0, CHUNKS, decode_and_add, 0)

    wait_bytes(from_pool.at[pl.ds(1, POOL - 1)], pool_recv)
    groups = row_group[...]

    def add_pool(i, carry):
        return jnp.where(
            groups == (me + POOL - i) % POOL, from_pool[i].astype(jnp.float32), carry
        )

    own = decoded[0].astype(jnp.float32)
    decode_out[...] = lax.fori_loop(1, POOL, add_pool, own).astype(jnp.bfloat16)

    def add_y(chunk, carry):
        wait_bytes(from_y.at[chunk, pl.ds(1, 3)], y_recv.at[chunk])
        rows = mid[chunk, pl.ds(y * 16, 16), :].astype(jnp.float32)
        for i in range(1, 4):
            rows = rows + from_y[chunk, i].astype(jnp.float32)
        out[:, pl.ds(pl.multiple_of(chunk * CHUNK, CHUNK), CHUNK)] = rows.astype(jnp.bfloat16)
        return carry

    lax.fori_loop(0, CHUNKS, add_y, 0)

    wait_bytes(pages_in.at[pl.ds(1, POOL - 1)], page_recv)
    wait_bytes(turn_in.at[pl.ds(1, 3)], turn_recv)
    wait_bytes(store.at[pl.ds(1, POOL - 1)], fetch_send)
    wait_bytes(cache_kv.at[pl.ds(0, TP - 1)], head_send)
    wait_bytes(turn_kv.at[pl.ds(0, TP - 1)], turn_head_send)
    wait_bytes(pages_out.at[pl.ds(1, POOL - 1)], page_send)
    wait_bytes(turn_out.at[pl.ds(1, 3)], turn_send)
    wait_bytes(gathered.at[0, pl.ds(0, 14)], ring_send)
    pair_copy.wait_send()
    wait_bytes(gathered.at[core], core_send)
    wait_bytes(decoded.at[pl.ds(1, POOL - 1)], pool_send)
    wait_bytes(from_x.at[:, pl.ds(1, 3)], x_send)
    wait_bytes(from_y.at[:, pl.ds(1, 3)], y_send)


def layer_call(*operands):
    vmem = pl.BlockSpec(memory_space=pltpu.VMEM)
    smem = pl.BlockSpec(memory_space=pltpu.SMEM)
    anywhere = pl.BlockSpec(memory_space=pl.ANY)
    dma = pltpu.SemaphoreType.DMA
    scratch = [
        (2, 16, BLOCK_ROWS, HEAD_SIZE),
        (POOL, 64, HEAD_SIZE),
        (KEY_VALUE_HEADS, 2, 128, HEAD_SIZE),
        (KEY_VALUE_HEADS, 2, TURN_ROWS, HEAD_SIZE),
        (TP, 2, 128, HEAD_SIZE),
        (TP, 2, TURN_ROWS, HEAD_SIZE),
        (POOL, PAGE_POSITIONS, HEAD_SIZE),
        (4, PAGE_POSITIONS, HEAD_SIZE),
        (512, 512),
        (1, KEYS),
        (TURN_TOKENS, HEADS_DEV * HEAD_SIZE),
        (POOL, QUERY_ROWS, HEAD_SIZE),
        (POOL, QUERY_ROWS, HEAD_SIZE),
        (CHUNKS, TURN_TOKENS, CHUNK),
        (CHUNKS, 4, 64, CHUNK),
        (CHUNKS, 64, CHUNK),
        (CHUNKS, 4, 16, CHUNK),
    ]
    return pl.pallas_call(
        layer_kernel,
        out_shape=(
            jax.ShapeDtypeStruct((16, CHUNKS * CHUNK), jnp.bfloat16),
            jax.ShapeDtypeStruct((QUERY_ROWS, HEAD_SIZE), jnp.bfloat16),
            jax.ShapeDtypeStruct((POOL, PAGE_POSITIONS, HEAD_SIZE), jnp.bfloat16),
            jax.ShapeDtypeStruct((4, PAGE_POSITIONS, HEAD_SIZE), jnp.bfloat16),
        ),
        in_specs=[smem, vmem, vmem, vmem, vmem, anywhere, vmem, vmem],
        out_specs=(vmem, vmem, vmem, vmem),
        scratch_shapes=[
            pltpu.VMEM(shape, jnp.float32 if shape == (1, KEYS) else jnp.bfloat16)
            for shape in scratch
        ]
        + [
            dma,
            dma((8,)),
            dma,
            dma,
            dma,
            dma,
            dma,
            dma,
            dma,
            dma,
            dma,
            dma((2, 4, 2)),
            dma,
            dma,
            dma,
            dma,
            dma((2,)),
            dma,
            dma,
            dma,
            dma((CHUNKS,)),
            dma,
            dma((CHUNKS,)),
        ],
        compiler_params=pltpu.CompilerParams(
            collective_id=0, has_side_effects=True, vmem_limit_bytes=VMEM_LIMIT
        ),
        name="attention_layer",
    )(*operands)


def cache_kernel(pages_in, turn_in, cache):
    me = lax.axis_index("pool")

    def one_request(request, carry):
        slot = (me - request + POOL) % POOL
        page = pages_in[slot]
        turn_page = turn_in[jnp.minimum(slot, 3)]
        turn_page = jnp.where(slot < 4, turn_page, jnp.zeros_like(turn_page))
        for kv in range(2):
            columns = slice(kv * 64, kv * 64 + 64)
            cache[0, request, 0, kv] = page[:, columns]
            cache[0, request, 1, kv] = turn_page[:, columns]
        return carry

    lax.fori_loop(0, POOL, one_request, 0)


def cache_call(pages_in, turn_in):
    vmem = pl.BlockSpec(memory_space=pltpu.VMEM)
    return pl.pallas_call(
        cache_kernel,
        out_shape=jax.ShapeDtypeStruct((1, POOL, 2, 2, PAGE_POSITIONS, 64), jnp.bfloat16),
        in_specs=[vmem, vmem],
        out_specs=vmem,
        compiler_params=pltpu.CompilerParams(vmem_limit_bytes=VMEM_LIMIT),
        name="decode_cache",
    )(pages_in, turn_in)


def per_device(
    turn_query_rows,
    turn_key_value,
    prefix_page_store,
    prefix_pages,
    holder_table,
    out_weight,
    row_request,
    step_query,
    step_kv,
):
    me = lax.axis_index("pool")
    rank = lax.axis_index("tp")
    store = prefix_page_store.reshape(POOL, 64, HEAD_SIZE)
    queries = jnp.transpose(
        step_query.reshape(DECODE_STEPS, 8, HEADS_DEV, HEAD_SIZE), (0, 2, 1, 3)
    ).reshape(QUERY_ROWS, HEAD_SIZE)
    fresh = lax.dynamic_slice_in_dim(step_kv, (rank // 2) * HEAD_SIZE, HEAD_SIZE, 3)
    fresh = jnp.transpose(fresh, (0, 2, 1, 3)).reshape(FRESH_ROWS, HEAD_SIZE)
    own_rows = lax.dynamic_slice_in_dim(row_request, me * 8, 8, 0)
    row_group = jnp.broadcast_to(own_rows[None], (8, 8)).reshape(QUERY_ROWS, 1)
    prefill_out, decode_rows, pages_in, turn_in = layer_call(
        prefix_pages,
        holder_table,
        row_group,
        store,
        turn_key_value.reshape(2, TURN_ROWS, KEY_VALUE_HEADS * HEAD_SIZE),
        out_weight,
        jnp.concatenate([queries, fresh], axis=0),
        turn_query_rows,
    )
    decode_out = jnp.transpose(
        decode_rows.reshape(DECODE_STEPS, HEADS_DEV, 8, HEAD_SIZE), (0, 2, 1, 3)
    ).reshape(DECODE_STEPS, 8, HEADS_DEV * HEAD_SIZE)
    return (prefill_out, decode_out, cache_call(pages_in, turn_in))


def solution(mesh):
    placed = (
        P("pool", "tp"),
        P("pool", None, "tp", None),
        P("pool", None, "tp", None),
        P(),
        P(),
        P("tp", "pool"),
        P(),
        P(None, "pool", "tp"),
        P(None, "pool", None, None),
    )
    return jax.shard_map(
        per_device,
        mesh=mesh,
        in_specs=placed,
        out_specs=(
            P(("pool", "tp"), None),
            P(None, "pool", "tp"),
            P("pool", None, None, None, None, "tp"),
        ),
        check_vma=False,
    )
```

```python
import math

import jax
import jax.numpy as jnp
from jax import lax
from jax.experimental import pallas as pl
from jax.experimental.pallas import tpu as pltpu
from jax.sharding import PartitionSpec as P

QUERY_HEADS = 64
KEY_VALUE_HEADS = 8
HEAD_SIZE = 128
PAGE_POSITIONS = 64
PREFIX_PAGE_CAP = 32
TURN_TOKENS = 256
DECODE_STEPS = 2
POOL = 32
TP = 16
HEADS_DEV = QUERY_HEADS // TP
SCORE_SCALE = 1.0 / math.sqrt(HEAD_SIZE)
EXP2_SCALE = SCORE_SCALE * math.log2(math.e)
WEIGHT_ROWS = 512
QUERY_ROWS = 64
FRESH_ROWS = 32
BLOCK_ROWS = WEIGHT_ROWS + QUERY_ROWS + FRESH_ROWS
TURN_ROWS = TURN_TOKENS // TP
KEYS = PREFIX_PAGE_CAP * PAGE_POSITIONS
CHUNKS = 4
CHUNK = 1024
VMEM_LIMIT = 56 * 1024 * 1024

MESH = pl.DeviceIdType.MESH
NT = (((1,), (1,)), ((), ()))


def remote(src, dst, send_sem, recv_sem, **axes):
    return pltpu.make_async_remote_copy(
        src_ref=src,
        dst_ref=dst,
        send_sem=send_sem,
        recv_sem=recv_sem,
        device_id=axes,
        device_id_type=MESH,
    )


def wait_bytes(like, sem):
    pltpu.make_async_copy(like, like, sem).wait()


def half_columns(keys, values, parity):
    low = lax.broadcasted_iota(jnp.int32, keys.shape, 1) < 64
    even = jnp.where(low, keys, pltpu.roll(values, 64, 1))
    odd = jnp.where(low, pltpu.roll(keys, 64, 1), values)
    return jnp.where(parity == 0, even, odd).astype(jnp.bfloat16)


def iota(shape, dimension):
    return lax.broadcasted_iota(jnp.int32, shape, dimension)


def one_hot(condition):
    return jnp.where(condition, 1.0, 0.0).astype(jnp.bfloat16)


def layer_kernel(
    prefix_pages,
    row_request,
    holder_table,
    store,
    turn,
    weight,
    step_query,
    fresh_rows_in,
    query,
    out,
    decode_out,
    pages_in,
    turn_in,
    gathered,
    rows_to_ring,
    fetched,
    by_head,
    turn_by_head,
    cache_kv,
    turn_kv,
    pages_out,
    turn_out,
    page_pick,
    live_bias,
    attention,
    decoded,
    from_pool,
    partial,
    from_x,
    mid,
    from_y,
    fetch_send,
    fetch_recv,
    head_send,
    head_recv,
    turn_head_send,
    turn_head_recv,
    page_send,
    page_recv,
    turn_send,
    turn_recv,
    ring_send,
    ring_recv,
    pair_send,
    pair_recv,
    core_send,
    core_recv,
    own_sem,
    pool_send,
    pool_recv,
    x_send,
    x_recv,
    y_send,
    y_recv,
):
    me = lax.axis_index("pool")
    rank = lax.axis_index("tp")
    z = me // 4
    y_hi = (me // 2) % 2
    core = me % 2
    x = rank // 4
    y = rank % 4
    other_core = me + 1 - 2 * core
    partner = me + 2 - 4 * y_hi

    barrier = pltpu.get_barrier_semaphore()

    def greet_pool(i, carry):
        pl.semaphore_signal(
            barrier, inc=1, device_id={"pool": (me + i) % POOL}, device_id_type=MESH
        )
        return carry

    def greet_tp(i, carry):
        pl.semaphore_signal(
            barrier, inc=1, device_id={"tp": (rank + i) % TP}, device_id_type=MESH
        )
        return carry

    lax.fori_loop(1, POOL, greet_pool, 0)
    lax.fori_loop(1, TP, greet_tp, 0)

    def place(at_z, at_y):
        return ((at_z + 8) % 8) * 2 + at_y

    own_place = place(z, y_hi)
    pair_place = place(z, 1 - y_hi)
    own_block = gathered.at[core, own_place]
    weight_copy = pltpu.make_async_copy(
        weight, own_block.at[pl.ds(0, WEIGHT_ROWS)], own_sem.at[0]
    )
    rows_copy = pltpu.make_async_copy(
        rows_to_ring, own_block.at[pl.ds(WEIGHT_ROWS, QUERY_ROWS + FRESH_ROWS)], own_sem.at[1]
    )
    weight_copy.start()
    for step in range(DECODE_STEPS):
        for pair in range(HEADS_DEV // 2):
            both = [
                step_query[step, :, head * HEAD_SIZE : (head + 1) * HEAD_SIZE]
                for head in (2 * pair, 2 * pair + 1)
            ]
            rows_to_ring[pl.ds(step * 32 + pair * 16, 16), :] = jnp.concatenate(both, axis=0)
    rows_to_ring[pl.ds(QUERY_ROWS, FRESH_ROWS), :] = fresh_rows_in[...]
    rows_copy.start()

    slots = (me + POOL - holder_table[pl.ds(me, 1), :]) % POOL
    square = (POOL, PREFIX_PAGE_CAP)
    slot_column = jnp.sum(
        jnp.where(iota(square, 0) == iota(square, 1), slots, 0), axis=1, keepdims=True
    )
    wide = (PREFIX_PAGE_CAP, 128)
    slot_live = jnp.max(
        jnp.where(
            (slot_column == iota(wide, 1) // 4) & (iota(wide, 0) < prefix_pages[me]), 1.0, 0.0
        ),
        axis=0,
        keepdims=True,
    )
    bias = jnp.where(slot_live > 0.0, 0.0, -jnp.inf)
    live_bias[...] = jnp.concatenate([bias] * TP, axis=1)
    tall = (512, PREFIX_PAGE_CAP)
    wanted_page = (iota(tall, 0) // 16 + POOL - me) % POOL
    row_slot = jnp.sum(
        jnp.where(iota(tall, 1) == wanted_page, slots, 0), axis=1, keepdims=True
    )
    row_code = row_slot * 16 + iota((512, 1), 0) % 16
    lane = iota((1, 512), 1)
    lane_code = ((lane % 128) // 4) * 16 + (lane // 128) * 4 + lane % 4
    page_pick[...] = one_hot(row_code == lane_code)
    mix_at = iota((128, 128), 0)
    mix = one_hot((mix_at % 16) * 8 + mix_at // 16 == iota((128, 128), 1))
    for kv in range(2):
        for head in range(KEY_VALUE_HEADS):
            turn_by_head[head, kv] = turn[kv, :, head * HEAD_SIZE : (head + 1) * HEAD_SIZE]
    weight_copy.wait()
    rows_copy.wait()

    pl.semaphore_wait(barrier, POOL - 1 + TP - 1)

    def fetch_copy(i):
        to = (me + i) % POOL
        return remote(
            store.at[to], fetched.at[i], fetch_send, fetch_recv.at[i // 4], pool=to
        )

    def start_fetch(i, carry):
        fetch_copy(i).start()
        return carry

    lax.fori_loop(1, POOL, start_fetch, 0)

    def ring_copy(direction, step, at_y):
        sign = 1 - 2 * direction
        slot = gathered.at[core, place(z - sign * step, at_y)]
        to = ((z + sign + 8) % 8) * 4 + y_hi * 2 + core
        return remote(slot, slot, ring_send, ring_recv.at[direction, step, at_y], pool=to)

    def core_copy(at):
        slot = gathered.at[core, at]
        return remote(slot, slot, core_send, core_recv, pool=other_core)

    def arrived(direction, step, at_y):
        sign = 1 - 2 * direction
        return place(z - sign * (step + 1), at_y)

    pair_copy = remote(own_block, own_block, pair_send, pair_recv, pool=partner)
    pair_copy.start()
    for direction in range(2):
        ring_copy(direction, 0, y_hi).start()

    def turn_head_copy(i):
        to = (rank + i) % TP
        return remote(
            turn_by_head.at[to // 2], turn_kv.at[rank], turn_head_send, turn_head_recv, tp=to
        )

    def start_turn_head(i, carry):
        turn_head_copy(i).start()
        return carry

    lax.fori_loop(1, TP, start_turn_head, 0)
    core_copy(own_place).start()
    fetched[0] = store[me]
    turn_kv[rank] = turn_by_head[rank // 2]

    def head_copy(i, part):
        to = (rank + i) % TP
        rows = pl.ds(part * 64, 64)
        return remote(
            by_head.at[to // 2, :, rows], cache_kv.at[rank, :, rows], head_send, head_recv, tp=to
        )

    def forward_pair():
        pair_copy.wait_recv()
        for direction in range(2):
            ring_copy(direction, 0, 1 - y_hi).start()
        core_copy(pair_place).start()

    def ring_step(step):
        for at_y in range(2):
            for direction in range(2):
                ring_copy(direction, step - 1, at_y).wait_recv()
                if step < 3 or at_y == direction:
                    ring_copy(direction, step, at_y).start()
                core_copy(arrived(direction, step - 1, at_y)).start()

    for part in range(2):

        def one_group(group, carry):
            rows = fetched[pl.ds(group * 4, 4)]
            for kv in range(2):
                moved = jnp.dot(
                    mix,
                    rows[:, kv * 32 : kv * 32 + 32].reshape(128, HEAD_SIZE),
                    preferred_element_type=jnp.float32,
                ).astype(jnp.bfloat16)
                by_head[:, kv, pl.ds(group * 16, 16), :] = moved.reshape(
                    KEY_VALUE_HEADS, 16, HEAD_SIZE
                )
            return carry

        def wait_group(group, carry):
            wait_bytes(fetched.at[pl.ds(group * 4, 4)], fetch_recv.at[group])
            return one_group(group, carry)

        if part == 0:
            wait_bytes(fetched.at[pl.ds(1, 3)], fetch_recv.at[0])
            one_group(0, 0)
            lax.fori_loop(1, 4, wait_group, 0)
        else:
            lax.fori_loop(4, 8, wait_group, 0)

        def start_head(i, carry):
            head_copy(i, part).start()
            return carry

        lax.fori_loop(1, TP, start_head, 0)
        if part == 0:
            forward_pair()
    cache_kv[rank] = by_head[rank // 2]
    ring_step(1)
    ring_step(2)
    ring_step(3)
    wait_bytes(cache_kv.at[pl.ds(0, TP - 1)], head_recv)
    wait_bytes(turn_kv.at[pl.ds(0, TP - 1)], turn_head_recv)

    parity = rank % 2

    def page_group(group, carry):
        members = pl.ds(group * 4, 4)
        rows = [
            cache_kv[members, kv].reshape(512, HEAD_SIZE).astype(jnp.float32) for kv in range(2)
        ]
        halves = half_columns(rows[0], rows[1], parity)
        picked = jnp.dot(page_pick[...], halves, preferred_element_type=jnp.float32)
        pages_out[:, pl.ds(group * 16, 16), :] = picked.astype(jnp.bfloat16).reshape(
            POOL, 16, HEAD_SIZE
        )
        rows = [
            turn_kv[members, kv].reshape(64, HEAD_SIZE).astype(jnp.float32) for kv in range(2)
        ]
        turn_out[group] = half_columns(rows[0], rows[1], parity)
        return carry

    lax.fori_loop(0, 4, page_group, 0)

    def start_page(i, carry):
        to = (me + i) % POOL
        remote(pages_out.at[to], pages_in.at[i], page_send, page_recv, pool=to).start()
        return carry

    def start_turn(i, carry):
        remote(
            turn_out.at[i], turn_in.at[i], turn_send, turn_recv, pool=(me + i) % POOL
        ).start()
        return carry

    lax.fori_loop(1, POOL, start_page, 0)
    lax.fori_loop(1, 4, start_turn, 0)
    pages_in[0] = pages_out[me]
    turn_in[0] = turn_out[0]

    def attend(rows, prefix_bias, turn_mask, fresh):
        scores = lax.dot_general(
            rows,
            cache_kv[:, 0].reshape(KEYS, HEAD_SIZE),
            NT,
            preferred_element_type=jnp.float32,
        )
        scores = scores + prefix_bias
        turn_scores = lax.dot_general(
            rows,
            turn_kv[:, 0].reshape(TURN_TOKENS, HEAD_SIZE),
            NT,
            preferred_element_type=jnp.float32,
        )
        if turn_mask is not None:
            turn_scores = jnp.where(turn_mask, turn_scores, -jnp.inf)
        top = jnp.maximum(
            jnp.max(scores, axis=1, keepdims=True), jnp.max(turn_scores, axis=1, keepdims=True)
        )
        for score, _ in fresh:
            top = jnp.maximum(top, score)
        top = top * EXP2_SCALE
        exponent = jnp.exp2(scores * EXP2_SCALE - top)
        turn_exponent = jnp.exp2(turn_scores * EXP2_SCALE - top)
        total = jnp.sum(exponent, axis=1, keepdims=True) + jnp.sum(
            turn_exponent, axis=1, keepdims=True
        )
        mixed = jnp.dot(
            exponent.astype(jnp.bfloat16),
            cache_kv[:, 1].reshape(KEYS, HEAD_SIZE),
            preferred_element_type=jnp.float32,
        ) + jnp.dot(
            turn_exponent.astype(jnp.bfloat16),
            turn_kv[:, 1].reshape(TURN_TOKENS, HEAD_SIZE),
            preferred_element_type=jnp.float32,
        )
        for score, value in fresh:
            share = jnp.exp2(score * EXP2_SCALE - top)
            total = total + share
            mixed = mixed + share * value
        return (mixed / total).astype(jnp.bfloat16)

    def attend_rows(half):
        causal = (128, TURN_TOKENS)
        at = iota(causal, 0)
        mask = iota(causal, 1) <= (at // 32) * 64 + half * 32 + at % 32
        for head in range(HEADS_DEV):
            columns = slice(head * HEAD_SIZE, (head + 1) * HEAD_SIZE)
            rows = query[:, half, :, columns].reshape(128, HEAD_SIZE)
            attention[:, columns] = attend(rows, live_bias[...], mask, ())

    def send_x(half, chunk, to):
        @pl.when(to != x)
        def _():
            slot = (to - x + 4) % 4
            remote(
                partial.at[half, chunk, to],
                from_x.at[half, chunk, slot],
                x_send,
                x_recv.at[half, chunk],
                tp=to * 4 + y,
            ).start()

    def project(half):
        def one_chunk(chunk, carry):
            def one_place(i, inner):
                both = [gathered[k, chunk * 4 + i, :WEIGHT_ROWS] for k in range(2)]
                product = jnp.dot(
                    attention[...],
                    jnp.concatenate(both, axis=1),
                    preferred_element_type=jnp.float32,
                )
                columns = pl.ds(pl.multiple_of(i * 256, 256), 256)
                partial[half, chunk, :, :, columns] = product.astype(jnp.bfloat16).reshape(
                    4, 32, 256
                )
                return inner

            lax.fori_loop(0, 4, one_place, 0)
            for i in (2, 1, 3):
                send_x(half, chunk, (x + i) % 4)
            return carry

        lax.fori_loop(0, CHUNKS, one_chunk, 0)

    for direction in range(2):
        ring_copy(direction, 3, direction).wait_recv()
        core_copy(arrived(direction, 3, direction)).start()
    attend_rows(0)
    wait_bytes(gathered.at[1 - core], core_recv)
    project(0)
    attend_rows(1)
    project(1)

    def decode_block(b, carry):
        part_core = b // 8
        places = pl.ds((b % 8) * 2, 2)
        rows = gathered[part_core, places, WEIGHT_ROWS : WEIGHT_ROWS + QUERY_ROWS].reshape(
            128, HEAD_SIZE
        )
        fresh_rows = (
            gathered[part_core, places, WEIGHT_ROWS + QUERY_ROWS :]
            .astype(jnp.float32)
            .reshape(2, 4, 1, 8, HEAD_SIZE)
        )
        rows_wide = rows.astype(jnp.float32)
        fresh = []
        for step in range(DECODE_STEPS):
            key, value = (
                jnp.broadcast_to(fresh_rows[:, 2 * step + kv], (2, 8, 8, HEAD_SIZE)).reshape(
                    128, HEAD_SIZE
                )
                for kv in range(2)
            )
            score = jnp.sum(rows_wide * key, axis=1, keepdims=True)
            if step == 1:
                score = jnp.where(iota((128, 1), 0) % 64 >= 32, score, -jnp.inf)
            fresh.append((score, value))
        result = attend(rows, live_bias[...], None, fresh).reshape(2, QUERY_ROWS, HEAD_SIZE)
        for k in range(2):
            to = ((b % 8) * 2 + k) * 2 + part_core
            slot = (to - me + POOL) % POOL
            decoded[slot] = result[k]

            @pl.when(slot > 0)
            def _():
                remote(
                    decoded.at[slot], from_pool.at[slot], pool_send, pool_recv, pool=to
                ).start()

        return carry

    def add_x(half, chunk):
        wait_bytes(from_x.at[half, chunk, pl.ds(1, 3)], x_recv.at[half, chunk])
        rows = partial[half, chunk, x].astype(jnp.float32)
        for i in range(1, 4):
            rows = rows + from_x[half, chunk, i].astype(jnp.float32)
        mid[half, chunk] = rows.astype(jnp.bfloat16)
        for k in range(2):
            to = half * 2 + k

            @pl.when(to != y)
            def _():
                remote(
                    mid.at[half, chunk, pl.ds(k * 16, 16)],
                    from_y.at[chunk, (to - y + 4) % 4],
                    y_send.at[half, k],
                    y_recv.at[chunk],
                    tp=x * 4 + to,
                ).start()

    def decode_and_add(i, carry):
        lax.fori_loop(2 * i, 2 * i + 2, decode_block, 0)
        add_x(i // CHUNKS, i % CHUNKS)
        return carry

    lax.fori_loop(0, 2 * CHUNKS, decode_and_add, 0)

    wait_bytes(from_pool.at[pl.ds(1, POOL - 1)], pool_recv)
    row_at = iota((QUERY_ROWS, HEAD_SIZE), 0) % 8
    groups = jnp.zeros((QUERY_ROWS, HEAD_SIZE), jnp.int32)
    for k in range(8):
        groups = jnp.where(row_at == k, row_request[me * 8 + k], groups)

    def add_pool(i, carry):
        return jnp.where(
            groups == (me + POOL - i) % POOL, from_pool[i].astype(jnp.float32), carry
        )

    own = decoded[0].astype(jnp.float32)
    decode_out[...] = lax.fori_loop(1, POOL, add_pool, own).astype(jnp.bfloat16)

    def add_y(chunk, carry):
        wait_bytes(from_y.at[chunk, pl.ds(1, 3)], y_recv.at[chunk])
        rows = mid[y // 2, chunk, pl.ds((y % 2) * 16, 16), :].astype(jnp.float32)
        for i in range(1, 4):
            rows = rows + from_y[chunk, i].astype(jnp.float32)
        out[:, pl.ds(pl.multiple_of(chunk * CHUNK, CHUNK), CHUNK)] = rows.astype(jnp.bfloat16)
        return carry

    lax.fori_loop(0, CHUNKS, add_y, 0)

    wait_bytes(pages_in.at[pl.ds(1, POOL - 1)], page_recv)
    wait_bytes(turn_in.at[pl.ds(1, 3)], turn_recv)
    wait_bytes(store.at[pl.ds(1, POOL - 1)], fetch_send)
    wait_bytes(cache_kv.at[pl.ds(0, TP - 1)], head_send)
    wait_bytes(turn_kv.at[pl.ds(0, TP - 1)], turn_head_send)
    wait_bytes(pages_out.at[pl.ds(1, POOL - 1)], page_send)
    wait_bytes(turn_out.at[pl.ds(1, 3)], turn_send)
    wait_bytes(gathered.at[0, pl.ds(0, 14)], ring_send)
    pair_copy.wait_send()
    wait_bytes(gathered.at[core], core_send)
    wait_bytes(decoded.at[pl.ds(1, POOL - 1)], pool_send)
    wait_bytes(from_x.at[:, :, pl.ds(1, 3)], x_send)
    for half in range(2):
        for k in range(2):

            @pl.when(half * 2 + k != y)
            def _():
                wait_bytes(from_y.at[:, 0], y_send.at[half, k])


def layer_call(*operands):
    vmem = pl.BlockSpec(memory_space=pltpu.VMEM)
    smem = pl.BlockSpec(memory_space=pltpu.SMEM)
    anywhere = pl.BlockSpec(memory_space=pl.ANY)
    dma = pltpu.SemaphoreType.DMA
    scratch = [
        (2, 16, BLOCK_ROWS, HEAD_SIZE),
        (QUERY_ROWS + FRESH_ROWS, HEAD_SIZE),
        (POOL, 64, HEAD_SIZE),
        (KEY_VALUE_HEADS, 2, 128, HEAD_SIZE),
        (KEY_VALUE_HEADS, 2, TURN_ROWS, HEAD_SIZE),
        (TP, 2, 128, HEAD_SIZE),
        (TP, 2, TURN_ROWS, HEAD_SIZE),
        (POOL, PAGE_POSITIONS, HEAD_SIZE),
        (4, PAGE_POSITIONS, HEAD_SIZE),
        (512, 512),
        (1, KEYS),
        (TURN_TOKENS // 2, HEADS_DEV * HEAD_SIZE),
        (POOL, QUERY_ROWS, HEAD_SIZE),
        (POOL, QUERY_ROWS, HEAD_SIZE),
        (2, CHUNKS, 4, 32, CHUNK),
        (2, CHUNKS, 4, 32, CHUNK),
        (2, CHUNKS, 32, CHUNK),
        (CHUNKS, 4, 16, CHUNK),
    ]
    return pl.pallas_call(
        layer_kernel,
        out_shape=(
            jax.ShapeDtypeStruct((16, CHUNKS * CHUNK), jnp.bfloat16),
            jax.ShapeDtypeStruct((QUERY_ROWS, HEAD_SIZE), jnp.bfloat16),
            jax.ShapeDtypeStruct((POOL, PAGE_POSITIONS, HEAD_SIZE), jnp.bfloat16),
            jax.ShapeDtypeStruct((4, PAGE_POSITIONS, HEAD_SIZE), jnp.bfloat16),
        ),
        in_specs=[smem, smem, vmem, vmem, vmem, anywhere, vmem, vmem, vmem],
        out_specs=(vmem, vmem, vmem, vmem),
        scratch_shapes=[
            pltpu.VMEM(shape, jnp.float32 if shape == (1, KEYS) else jnp.bfloat16)
            for shape in scratch
        ]
        + [
            dma,
            dma((8,)),
            dma,
            dma,
            dma,
            dma,
            dma,
            dma,
            dma,
            dma,
            dma,
            dma((2, 4, 2)),
            dma,
            dma,
            dma,
            dma,
            dma((2,)),
            dma,
            dma,
            dma,
            dma((2, CHUNKS)),
            dma((2, 2)),
            dma((CHUNKS,)),
        ],
        compiler_params=pltpu.CompilerParams(
            collective_id=0, has_side_effects=True, vmem_limit_bytes=VMEM_LIMIT
        ),
        name="attention_layer",
    )(*operands)


CACHE_STEP = 8


def cache_kernel(pages_in, turn_in, cache):
    me = lax.axis_index("pool")
    first = pl.program_id(0) * CACHE_STEP

    for k in range(CACHE_STEP):
        slot = (me - first - k + 2 * POOL) % POOL
        page = pages_in[slot]
        turn_page = turn_in[jnp.minimum(slot, 3)]
        turn_page = jnp.where(slot < 4, turn_page, jnp.zeros_like(turn_page))
        for kv in range(2):
            columns = slice(kv * 64, kv * 64 + 64)
            cache[0, k, 0, kv] = page[:, columns]
            cache[0, k, 1, kv] = turn_page[:, columns]


def cache_call(pages_in, turn_in):
    vmem = pl.BlockSpec(memory_space=pltpu.VMEM)
    tail = (2, 2, PAGE_POSITIONS, 64)
    return pl.pallas_call(
        cache_kernel,
        grid=(POOL // CACHE_STEP,),
        out_shape=jax.ShapeDtypeStruct((1, POOL) + tail, jnp.bfloat16),
        in_specs=[vmem, vmem],
        out_specs=pl.BlockSpec((1, CACHE_STEP) + tail, lambda i: (0, i, 0, 0, 0, 0)),
        compiler_params=pltpu.CompilerParams(vmem_limit_bytes=VMEM_LIMIT),
        name="decode_cache",
    )(pages_in, turn_in)


def per_device(
    turn_query_rows,
    turn_key_value,
    prefix_page_store,
    prefix_pages,
    holder_table,
    out_weight,
    row_request,
    step_query,
    step_kv,
):
    rank = lax.axis_index("tp")
    store = prefix_page_store.reshape(POOL, 64, HEAD_SIZE)
    fresh = lax.dynamic_slice_in_dim(step_kv, (rank // 2) * HEAD_SIZE, HEAD_SIZE, 3)
    fresh = jnp.transpose(fresh, (0, 2, 1, 3)).reshape(FRESH_ROWS, HEAD_SIZE)
    prefill_out, decode_rows, pages_in, turn_in = layer_call(
        prefix_pages,
        row_request,
        holder_table,
        store,
        turn_key_value.reshape(2, TURN_ROWS, KEY_VALUE_HEADS * HEAD_SIZE),
        out_weight,
        step_query,
        fresh,
        turn_query_rows.reshape(4, 2, 32, HEADS_DEV * HEAD_SIZE),
    )
    decode_out = jnp.transpose(
        decode_rows.reshape(DECODE_STEPS, HEADS_DEV, 8, HEAD_SIZE), (0, 2, 1, 3)
    ).reshape(DECODE_STEPS, 8, HEADS_DEV * HEAD_SIZE)
    return (prefill_out, decode_out, cache_call(pages_in, turn_in))


def solution(mesh):
    placed = (
        P("pool", "tp"),
        P("pool", None, "tp", None),
        P("pool", None, "tp", None),
        P(),
        P(),
        P("tp", "pool"),
        P(),
        P(None, "pool", "tp"),
        P(None, "pool", None, None),
    )
    return jax.shard_map(
        per_device,
        mesh=mesh,
        in_specs=placed,
        out_specs=(
            P(("pool", "tp"), None),
            P(None, "pool", "tp"),
            P("pool", None, None, None, None, "tp"),
        ),
        check_vma=False,
    )
```

```python
import math

import jax
import jax.numpy as jnp
from jax import lax
from jax.experimental import pallas as pl
from jax.experimental.pallas import tpu as pltpu
from jax.sharding import PartitionSpec as P

QUERY_HEADS = 64
KEY_VALUE_HEADS = 8
HEAD_SIZE = 128
PAGE_POSITIONS = 64
PREFIX_PAGE_CAP = 32
TURN_TOKENS = 256
DECODE_STEPS = 2
POOL = 32
TP = 16
HEADS_DEV = QUERY_HEADS // TP
SCORE_SCALE = 1.0 / math.sqrt(HEAD_SIZE)
EXP2_SCALE = SCORE_SCALE * math.log2(math.e)
WEIGHT_ROWS = 512
QUERY_ROWS = 64
FRESH_ROWS = 32
BLOCK_ROWS = WEIGHT_ROWS + QUERY_ROWS + FRESH_ROWS
TURN_ROWS = TURN_TOKENS // TP
KEYS = PREFIX_PAGE_CAP * PAGE_POSITIONS
GROUP_ROWS = 512
CHUNKS = 4
CHUNK = 1024
VMEM_LIMIT = 56 * 1024 * 1024

MESH = pl.DeviceIdType.MESH
NT = (((1,), (1,)), ((), ()))
TN = (((0,), (0,)), ((), ()))


def remote(src, dst, send_sem, recv_sem, **axes):
    return pltpu.make_async_remote_copy(
        src_ref=src,
        dst_ref=dst,
        send_sem=send_sem,
        recv_sem=recv_sem,
        device_id=axes,
        device_id_type=MESH,
    )


def wait_bytes(like, sem):
    pltpu.make_async_copy(like, like, sem).wait()


def half_columns(keys, values, parity):
    low = lax.broadcasted_iota(jnp.int32, keys.shape, 1) < 64
    even = jnp.where(low, keys, pltpu.roll(values, 64, 1))
    odd = jnp.where(low, pltpu.roll(keys, 64, 1), values)
    return jnp.where(parity == 0, even, odd).astype(jnp.bfloat16)


def iota(shape, dimension):
    return lax.broadcasted_iota(jnp.int32, shape, dimension)


def one_hot(condition):
    return jnp.where(condition, 1.0, 0.0).astype(jnp.bfloat16)


def layer_kernel(
    prefix_pages,
    row_request,
    holder_table,
    store,
    turn,
    weight,
    step_query,
    fresh_rows_in,
    query,
    out,
    decode_out,
    pages_in,
    turn_in,
    gathered,
    rows_to_ring,
    fetched,
    by_head,
    turn_by_head,
    cache_kv,
    turn_kv,
    pages_out,
    turn_out,
    page_pick,
    live_bias,
    attention,
    decoded,
    from_pool,
    partial,
    from_x,
    mid,
    from_y,
    fetch_send,
    fetch_recv,
    head_send,
    head_recv,
    turn_head_send,
    turn_head_recv,
    page_send,
    page_recv,
    turn_send,
    turn_recv,
    ring_send,
    ring_recv,
    pair_send,
    pair_recv,
    core_send,
    core_recv,
    own_sem,
    pool_send,
    pool_recv,
    x_send,
    x_recv,
    y_send,
    y_recv,
):
    me = lax.axis_index("pool")
    rank = lax.axis_index("tp")
    z = me // 4
    y_hi = (me // 2) % 2
    core = me % 2
    x = rank // 4
    y = rank % 4
    other_core = me + 1 - 2 * core
    partner = me + 2 - 4 * y_hi

    barrier = pltpu.get_barrier_semaphore()

    def greet_pool(i, carry):
        pl.semaphore_signal(
            barrier, inc=1, device_id={"pool": (me + i) % POOL}, device_id_type=MESH
        )
        return carry

    def greet_tp(i, carry):
        pl.semaphore_signal(
            barrier, inc=1, device_id={"tp": (rank + i) % TP}, device_id_type=MESH
        )
        return carry

    lax.fori_loop(1, POOL, greet_pool, 0)
    lax.fori_loop(1, TP, greet_tp, 0)

    def place(at_z, at_y):
        return ((at_z + 8) % 8) * 2 + at_y

    own_place = place(z, y_hi)
    pair_place = place(z, 1 - y_hi)
    own_block = gathered.at[core, own_place]
    weight_copy = pltpu.make_async_copy(
        weight, own_block.at[pl.ds(0, WEIGHT_ROWS)], own_sem.at[0]
    )
    rows_copy = pltpu.make_async_copy(
        rows_to_ring, own_block.at[pl.ds(WEIGHT_ROWS, QUERY_ROWS + FRESH_ROWS)], own_sem.at[1]
    )
    weight_copy.start()
    for step in range(DECODE_STEPS):
        for pair in range(HEADS_DEV // 2):
            both = [
                step_query[step, :, head * HEAD_SIZE : (head + 1) * HEAD_SIZE]
                for head in (2 * pair, 2 * pair + 1)
            ]
            rows_to_ring[pl.ds(step * 32 + pair * 16, 16), :] = jnp.concatenate(both, axis=0)
    rows_to_ring[pl.ds(QUERY_ROWS, FRESH_ROWS), :] = fresh_rows_in[...]
    rows_copy.start()

    slots = (me + POOL - holder_table[pl.ds(me, 1), :]) % POOL
    wide = (128, PREFIX_PAGE_CAP)
    slot_live = jnp.max(
        jnp.where((slots == iota(wide, 0) // 4) & (iota(wide, 1) < prefix_pages[me]), 1.0, 0.0),
        axis=1,
        keepdims=True,
    )
    live_bias[...] = jnp.broadcast_to(
        jnp.where(slot_live > 0.0, 0.0, -jnp.inf), live_bias.shape
    )
    tall = (512, PREFIX_PAGE_CAP)
    wanted_page = (iota(tall, 0) // 16 + POOL - me) % POOL
    row_slot = jnp.sum(
        jnp.where(iota(tall, 1) == wanted_page, slots, 0), axis=1, keepdims=True
    )
    row_code = row_slot * 16 + iota((512, 1), 0) % 16
    lane = iota((1, 512), 1)
    lane_code = ((lane % 128) // 4) * 16 + (lane // 128) * 4 + lane % 4
    page_pick[...] = one_hot(row_code == lane_code)
    mix_at = iota((128, 128), 0)
    mix = one_hot((mix_at % 16) * 8 + mix_at // 16 == iota((128, 128), 1))
    for kv in range(2):
        for head in range(KEY_VALUE_HEADS):
            turn_by_head[head, kv] = turn[kv, :, head * HEAD_SIZE : (head + 1) * HEAD_SIZE]
    weight_copy.wait()
    rows_copy.wait()

    pl.semaphore_wait(barrier, POOL - 1 + TP - 1)

    def fetch_copy(i):
        to = (me + i) % POOL
        return remote(
            store.at[to], fetched.at[i], fetch_send, fetch_recv.at[i // 4], pool=to
        )

    def start_fetch(i, carry):
        fetch_copy(i).start()
        return carry

    lax.fori_loop(1, POOL, start_fetch, 0)

    def ring_copy(direction, step, at_y):
        sign = 1 - 2 * direction
        slot = gathered.at[core, place(z - sign * step, at_y)]
        to = ((z + sign + 8) % 8) * 4 + y_hi * 2 + core
        return remote(slot, slot, ring_send, ring_recv.at[direction, step, at_y], pool=to)

    def core_copy(at):
        slot = gathered.at[core, at]
        return remote(slot, slot, core_send, core_recv, pool=other_core)

    def arrived(direction, step, at_y):
        sign = 1 - 2 * direction
        return place(z - sign * (step + 1), at_y)

    pair_copy = remote(own_block, own_block, pair_send, pair_recv, pool=partner)
    pair_copy.start()
    for direction in range(2):
        ring_copy(direction, 0, y_hi).start()

    def turn_head_copy(i):
        to = (rank + i) % TP
        return remote(
            turn_by_head.at[to // 2], turn_kv.at[rank], turn_head_send, turn_head_recv, tp=to
        )

    def start_turn_head(i, carry):
        turn_head_copy(i).start()
        return carry

    lax.fori_loop(1, TP, start_turn_head, 0)
    core_copy(own_place).start()
    fetched[0] = store[me]
    turn_kv[rank] = turn_by_head[rank // 2]

    def head_copy(i, part):
        to = (rank + i) % TP
        rows = pl.ds(part * 64, 64)
        return remote(
            by_head.at[to // 2, :, rows], cache_kv.at[rank, :, rows], head_send, head_recv, tp=to
        )

    def forward_pair():
        pair_copy.wait_recv()
        for direction in range(2):
            ring_copy(direction, 0, 1 - y_hi).start()
        core_copy(pair_place).start()

    def ring_step(step):
        for at_y in range(2):
            for direction in range(2):
                ring_copy(direction, step - 1, at_y).wait_recv()
                if step < 3 or at_y == direction:
                    ring_copy(direction, step, at_y).start()
                core_copy(arrived(direction, step - 1, at_y)).start()

    for part in range(2):

        def one_group(group, carry):
            rows = fetched[pl.ds(group * 4, 4)]
            for kv in range(2):
                moved = jnp.dot(
                    mix,
                    rows[:, kv * 32 : kv * 32 + 32].reshape(128, HEAD_SIZE),
                    preferred_element_type=jnp.float32,
                ).astype(jnp.bfloat16)
                by_head[:, kv, pl.ds(group * 16, 16), :] = moved.reshape(
                    KEY_VALUE_HEADS, 16, HEAD_SIZE
                )
            return carry

        def wait_group(group, carry):
            wait_bytes(fetched.at[pl.ds(group * 4, 4)], fetch_recv.at[group])
            return one_group(group, carry)

        if part == 0:
            wait_bytes(fetched.at[pl.ds(1, 3)], fetch_recv.at[0])
            one_group(0, 0)
            lax.fori_loop(1, 4, wait_group, 0)
        else:
            lax.fori_loop(4, 8, wait_group, 0)

        def start_head(i, carry):
            head_copy(i, part).start()
            return carry

        lax.fori_loop(1, TP, start_head, 0)
        if part == 0:
            forward_pair()
    cache_kv[rank] = by_head[rank // 2]
    ring_step(1)
    ring_step(2)
    ring_step(3)
    wait_bytes(cache_kv.at[pl.ds(0, TP - 1)], head_recv)
    wait_bytes(turn_kv.at[pl.ds(0, TP - 1)], turn_head_recv)

    parity = rank % 2

    def page_group(group, carry):
        members = pl.ds(group * 4, 4)
        rows = [
            cache_kv[members, kv].reshape(512, HEAD_SIZE).astype(jnp.float32) for kv in range(2)
        ]
        halves = half_columns(rows[0], rows[1], parity)
        picked = jnp.dot(page_pick[...], halves, preferred_element_type=jnp.float32)
        pages_out[:, pl.ds(group * 16, 16), :] = picked.astype(jnp.bfloat16).reshape(
            POOL, 16, HEAD_SIZE
        )
        rows = [
            turn_kv[members, kv].reshape(64, HEAD_SIZE).astype(jnp.float32) for kv in range(2)
        ]
        turn_out[group] = half_columns(rows[0], rows[1], parity)
        return carry

    lax.fori_loop(0, 4, page_group, 0)

    def start_page(i, carry):
        to = (me + i) % POOL
        remote(pages_out.at[to], pages_in.at[i], page_send, page_recv, pool=to).start()
        return carry

    def start_turn(i, carry):
        remote(
            turn_out.at[i], turn_in.at[i], turn_send, turn_recv, pool=(me + i) % POOL
        ).start()
        return carry

    lax.fori_loop(1, POOL, start_page, 0)
    lax.fori_loop(1, 4, start_turn, 0)
    pages_in[0] = pages_out[me]
    turn_in[0] = turn_out[0]

    def attend(rows, turn_mask, fresh):
        scores = lax.dot_general(
            cache_kv[:, 0].reshape(KEYS, HEAD_SIZE),
            rows,
            NT,
            preferred_element_type=jnp.float32,
        )
        bias = jnp.concatenate([live_bias[...]] * (GROUP_ROWS // 128), axis=1)
        scores = (scores.reshape(TP, 128, GROUP_ROWS) + bias[None]).reshape(KEYS, GROUP_ROWS)
        turn_scores = lax.dot_general(
            turn_kv[:, 0].reshape(TURN_TOKENS, HEAD_SIZE),
            rows,
            NT,
            preferred_element_type=jnp.float32,
        )
        if turn_mask is not None:
            turn_scores = jnp.where(turn_mask, turn_scores, -jnp.inf)
        top = jnp.maximum(
            jnp.max(scores, axis=0, keepdims=True), jnp.max(turn_scores, axis=0, keepdims=True)
        )
        for score, _ in fresh:
            top = jnp.maximum(top, score)
        top = top * EXP2_SCALE
        exponent = jnp.exp2(scores * EXP2_SCALE - top)
        turn_exponent = jnp.exp2(turn_scores * EXP2_SCALE - top)
        total = jnp.sum(exponent, axis=0, keepdims=True) + jnp.sum(
            turn_exponent, axis=0, keepdims=True
        )
        mixed = lax.dot_general(
            cache_kv[:, 1].reshape(KEYS, HEAD_SIZE),
            exponent.astype(jnp.bfloat16),
            TN,
            preferred_element_type=jnp.float32,
        ) + lax.dot_general(
            turn_kv[:, 1].reshape(TURN_TOKENS, HEAD_SIZE),
            turn_exponent.astype(jnp.bfloat16),
            TN,
            preferred_element_type=jnp.float32,
        )
        for score, value in fresh:
            share = jnp.exp2(score * EXP2_SCALE - top)
            total = total + share
            mixed = mixed + share * value
        return (mixed / total).T.astype(jnp.bfloat16)

    def attend_rows(half):
        causal = (TURN_TOKENS, GROUP_ROWS)
        at = iota(causal, 1) % 128
        mask = iota(causal, 0) <= (at // 32) * 64 + half * 32 + at % 32
        heads = [slice(head * HEAD_SIZE, (head + 1) * HEAD_SIZE) for head in range(HEADS_DEV)]
        rows = [query[:, half, :, columns].reshape(128, HEAD_SIZE) for columns in heads]
        result = attend(jnp.concatenate(rows, axis=0), mask, ())
        for head, columns in enumerate(heads):
            attention[:, columns] = result[head * 128 : (head + 1) * 128]

    def send_x(half, chunk, to):
        @pl.when(to != x)
        def _():
            slot = (to - x + 4) % 4
            remote(
                partial.at[half, chunk, to],
                from_x.at[half, chunk, slot],
                x_send,
                x_recv.at[half, chunk],
                tp=to * 4 + y,
            ).start()

    def project(half):
        def one_chunk(chunk, carry):
            def one_place(i, inner):
                both = [gathered[k, chunk * 4 + i, :WEIGHT_ROWS] for k in range(2)]
                product = jnp.dot(
                    attention[...],
                    jnp.concatenate(both, axis=1),
                    preferred_element_type=jnp.float32,
                )
                columns = pl.ds(pl.multiple_of(i * 256, 256), 256)
                partial[half, chunk, :, :, columns] = product.astype(jnp.bfloat16).reshape(
                    4, 32, 256
                )
                return inner

            lax.fori_loop(0, 4, one_place, 0)
            for i in (2, 1, 3):
                send_x(half, chunk, (x + i) % 4)
            return carry

        lax.fori_loop(0, CHUNKS, one_chunk, 0)

    for direction in range(2):
        ring_copy(direction, 3, direction).wait_recv()
        core_copy(arrived(direction, 3, direction)).start()
    attend_rows(0)
    wait_bytes(gathered.at[1 - core], core_recv)
    project(0)
    attend_rows(1)
    project(1)

    def decode_block(b):
        part_core = b // 2
        places = pl.ds((b % 2) * 8, 8)
        rows = gathered[part_core, places, WEIGHT_ROWS : WEIGHT_ROWS + QUERY_ROWS].reshape(
            GROUP_ROWS, HEAD_SIZE
        )
        fresh_rows = (
            gathered[part_core, places, WEIGHT_ROWS + QUERY_ROWS :]
            .astype(jnp.float32)
            .reshape(8, 4, 1, 8, HEAD_SIZE)
        )
        rows_wide = rows.astype(jnp.float32)
        fresh = []
        for step in range(DECODE_STEPS):
            key, value = (
                jnp.broadcast_to(fresh_rows[:, 2 * step + kv], (8, 8, 8, HEAD_SIZE)).reshape(
                    GROUP_ROWS, HEAD_SIZE
                )
                for kv in range(2)
            )
            score = jnp.sum((rows_wide * key).T, axis=0, keepdims=True)
            if step == 1:
                score = jnp.where(iota((1, GROUP_ROWS), 1) % 64 >= 32, score, -jnp.inf)
            fresh.append((score, value.T))
        result = attend(rows, None, fresh).reshape(8, QUERY_ROWS, HEAD_SIZE)
        for k in range(8):
            to = ((b % 2) * 8 + k) * 2 + part_core
            slot = (to - me + POOL) % POOL
            decoded[slot] = result[k]

            @pl.when(slot > 0)
            def _():
                remote(
                    decoded.at[slot], from_pool.at[slot], pool_send, pool_recv, pool=to
                ).start()

    def add_x(half, chunk):
        wait_bytes(from_x.at[half, chunk, pl.ds(1, 3)], x_recv.at[half, chunk])
        rows = partial[half, chunk, x].astype(jnp.float32)
        for i in range(1, 4):
            rows = rows + from_x[half, chunk, i].astype(jnp.float32)
        mid[half, chunk] = rows.astype(jnp.bfloat16)
        for k in range(2):
            to = half * 2 + k

            @pl.when(to != y)
            def _():
                remote(
                    mid.at[half, chunk, pl.ds(k * 16, 16)],
                    from_y.at[chunk, (to - y + 4) % 4],
                    y_send.at[half, k],
                    y_recv.at[chunk],
                    tp=x * 4 + to,
                ).start()

    def decode_and_add(i, carry):
        decode_block(i)
        add_x(i // 2, (i % 2) * 2)
        add_x(i // 2, (i % 2) * 2 + 1)
        return carry

    lax.fori_loop(0, 4, decode_and_add, 0)

    wait_bytes(from_pool.at[pl.ds(1, POOL - 1)], pool_recv)
    row_at = iota((QUERY_ROWS, HEAD_SIZE), 0) % 8
    groups = jnp.zeros((QUERY_ROWS, HEAD_SIZE), jnp.int32)
    for k in range(8):
        groups = jnp.where(row_at == k, row_request[me * 8 + k], groups)

    def add_pool(i, carry):
        return jnp.where(
            groups == (me + POOL - i) % POOL, from_pool[i].astype(jnp.float32), carry
        )

    own = decoded[0].astype(jnp.float32)
    decode_out[...] = lax.fori_loop(1, POOL, add_pool, own).astype(jnp.bfloat16)

    def add_y(chunk, carry):
        wait_bytes(from_y.at[chunk, pl.ds(1, 3)], y_recv.at[chunk])
        rows = mid[y // 2, chunk, pl.ds((y % 2) * 16, 16), :].astype(jnp.float32)
        for i in range(1, 4):
            rows = rows + from_y[chunk, i].astype(jnp.float32)
        out[:, pl.ds(pl.multiple_of(chunk * CHUNK, CHUNK), CHUNK)] = rows.astype(jnp.bfloat16)
        return carry

    lax.fori_loop(0, CHUNKS, add_y, 0)

    wait_bytes(pages_in.at[pl.ds(1, POOL - 1)], page_recv)
    wait_bytes(turn_in.at[pl.ds(1, 3)], turn_recv)
    wait_bytes(store.at[pl.ds(1, POOL - 1)], fetch_send)
    wait_bytes(cache_kv.at[pl.ds(0, TP - 1)], head_send)
    wait_bytes(turn_kv.at[pl.ds(0, TP - 1)], turn_head_send)
    wait_bytes(pages_out.at[pl.ds(1, POOL - 1)], page_send)
    wait_bytes(turn_out.at[pl.ds(1, 3)], turn_send)
    wait_bytes(gathered.at[0, pl.ds(0, 14)], ring_send)
    pair_copy.wait_send()
    wait_bytes(gathered.at[core], core_send)
    wait_bytes(decoded.at[pl.ds(1, POOL - 1)], pool_send)
    wait_bytes(from_x.at[:, :, pl.ds(1, 3)], x_send)
    for half in range(2):
        for k in range(2):

            @pl.when(half * 2 + k != y)
            def _():
                wait_bytes(from_y.at[:, 0], y_send.at[half, k])


def layer_call(*operands):
    vmem = pl.BlockSpec(memory_space=pltpu.VMEM)
    smem = pl.BlockSpec(memory_space=pltpu.SMEM)
    anywhere = pl.BlockSpec(memory_space=pl.ANY)
    dma = pltpu.SemaphoreType.DMA
    scratch = [
        (2, 16, BLOCK_ROWS, HEAD_SIZE),
        (QUERY_ROWS + FRESH_ROWS, HEAD_SIZE),
        (POOL, 64, HEAD_SIZE),
        (KEY_VALUE_HEADS, 2, 128, HEAD_SIZE),
        (KEY_VALUE_HEADS, 2, TURN_ROWS, HEAD_SIZE),
        (TP, 2, 128, HEAD_SIZE),
        (TP, 2, TURN_ROWS, HEAD_SIZE),
        (POOL, PAGE_POSITIONS, HEAD_SIZE),
        (4, PAGE_POSITIONS, HEAD_SIZE),
        (512, 512),
        (128, 128),
        (TURN_TOKENS // 2, HEADS_DEV * HEAD_SIZE),
        (POOL, QUERY_ROWS, HEAD_SIZE),
        (POOL, QUERY_ROWS, HEAD_SIZE),
        (2, CHUNKS, 4, 32, CHUNK),
        (2, CHUNKS, 4, 32, CHUNK),
        (2, CHUNKS, 32, CHUNK),
        (CHUNKS, 4, 16, CHUNK),
    ]
    return pl.pallas_call(
        layer_kernel,
        out_shape=(
            jax.ShapeDtypeStruct((16, CHUNKS * CHUNK), jnp.bfloat16),
            jax.ShapeDtypeStruct((QUERY_ROWS, HEAD_SIZE), jnp.bfloat16),
            jax.ShapeDtypeStruct((POOL, PAGE_POSITIONS, HEAD_SIZE), jnp.bfloat16),
            jax.ShapeDtypeStruct((4, PAGE_POSITIONS, HEAD_SIZE), jnp.bfloat16),
        ),
        in_specs=[smem, smem, vmem, vmem, vmem, anywhere, vmem, vmem, vmem],
        out_specs=(vmem, vmem, vmem, vmem),
        scratch_shapes=[
            pltpu.VMEM(shape, jnp.float32 if shape == (128, 128) else jnp.bfloat16)
            for shape in scratch
        ]
        + [
            dma,
            dma((8,)),
            dma,
            dma,
            dma,
            dma,
            dma,
            dma,
            dma,
            dma,
            dma,
            dma((2, 4, 2)),
            dma,
            dma,
            dma,
            dma,
            dma((2,)),
            dma,
            dma,
            dma,
            dma((2, CHUNKS)),
            dma((2, 2)),
            dma((CHUNKS,)),
        ],
        compiler_params=pltpu.CompilerParams(
            collective_id=0, has_side_effects=True, vmem_limit_bytes=VMEM_LIMIT
        ),
        name="attention_layer",
    )(*operands)


CACHE_STEP = 8


def last_kernel(pages_in, turn_in, prefill_in, decode_in, cache, prefill_out, decode_out):
    me = lax.axis_index("pool")
    first = pl.program_id(0) * CACHE_STEP

    @pl.when(first == 0)
    def _():
        prefill_out[...] = prefill_in[...]
        for step in range(DECODE_STEPS):
            for head in range(HEADS_DEV):
                rows = decode_in[step * 32 + head * 8 : step * 32 + head * 8 + 8]
                decode_out[step, :, head * HEAD_SIZE : (head + 1) * HEAD_SIZE] = rows

    for k in range(CACHE_STEP):
        slot = (me - first - k + 2 * POOL) % POOL
        page = pages_in[slot]
        turn_page = turn_in[jnp.minimum(slot, 3)]
        turn_page = jnp.where(slot < 4, turn_page, jnp.zeros_like(turn_page))
        for kv in range(2):
            columns = slice(kv * 64, kv * 64 + 64)
            cache[0, k, 0, kv] = page[:, columns]
            cache[0, k, 1, kv] = turn_page[:, columns]


def last_call(pages_in, turn_in, prefill, decoded):
    vmem = pl.BlockSpec(memory_space=pltpu.VMEM)
    tail = (2, 2, PAGE_POSITIONS, 64)
    decode_shape = (DECODE_STEPS, 8, HEADS_DEV * HEAD_SIZE)
    return pl.pallas_call(
        last_kernel,
        grid=(POOL // CACHE_STEP,),
        out_shape=(
            jax.ShapeDtypeStruct((1, POOL) + tail, jnp.bfloat16),
            jax.ShapeDtypeStruct(prefill.shape, jnp.bfloat16),
            jax.ShapeDtypeStruct(decode_shape, jnp.bfloat16),
        ),
        in_specs=[vmem] * 4,
        out_specs=(
            pl.BlockSpec((1, CACHE_STEP) + tail, lambda i: (0, i, 0, 0, 0, 0)),
            pl.BlockSpec(prefill.shape, lambda i: (0, 0)),
            pl.BlockSpec(decode_shape, lambda i: (0, 0, 0)),
        ),
        compiler_params=pltpu.CompilerParams(vmem_limit_bytes=VMEM_LIMIT),
        name="lay_out_results",
    )(pages_in, turn_in, prefill, decoded)


def per_device(
    turn_query_rows,
    turn_key_value,
    prefix_page_store,
    prefix_pages,
    holder_table,
    out_weight,
    row_request,
    step_query,
    step_kv,
):
    rank = lax.axis_index("tp")
    store = prefix_page_store.reshape(POOL, 64, HEAD_SIZE)
    fresh = lax.dynamic_slice_in_dim(step_kv, (rank // 2) * HEAD_SIZE, HEAD_SIZE, 3)
    fresh = jnp.transpose(fresh, (0, 2, 1, 3)).reshape(FRESH_ROWS, HEAD_SIZE)
    prefill_out, decode_rows, pages_in, turn_in = layer_call(
        prefix_pages,
        row_request,
        holder_table,
        store,
        turn_key_value.reshape(2, TURN_ROWS, KEY_VALUE_HEADS * HEAD_SIZE),
        out_weight,
        step_query,
        fresh,
        turn_query_rows.reshape(4, 2, 32, HEADS_DEV * HEAD_SIZE),
    )
    decode_cache, prefill_out, decode_out = last_call(
        pages_in, turn_in, prefill_out, decode_rows
    )
    return (prefill_out, decode_out, decode_cache)


def solution(mesh):
    placed = (
        P("pool", "tp"),
        P("pool", None, "tp", None),
        P("pool", None, "tp", None),
        P(),
        P(),
        P("tp", "pool"),
        P(),
        P(None, "pool", "tp"),
        P(None, "pool", None, None),
    )
    return jax.shard_map(
        per_device,
        mesh=mesh,
        in_specs=placed,
        out_specs=(
            P(("pool", "tp"), None),
            P(None, "pool", "tp"),
            P("pool", None, None, None, None, "tp"),
        ),
        check_vma=False,
    )
```

```python
import math

import jax
import jax.numpy as jnp
from jax import lax
from jax.experimental import pallas as pl
from jax.experimental.pallas import tpu as pltpu
from jax.sharding import PartitionSpec as P

QUERY_HEADS = 64
KEY_VALUE_HEADS = 8
HEAD_SIZE = 128
PAGE_POSITIONS = 64
PREFIX_PAGE_CAP = 32
TURN_TOKENS = 256
DECODE_STEPS = 2
POOL = 32
TP = 16
HEADS_DEV = QUERY_HEADS // TP
SCORE_SCALE = 1.0 / math.sqrt(HEAD_SIZE)
EXP2_SCALE = SCORE_SCALE * math.log2(math.e)
WEIGHT_ROWS = 512
QUERY_ROWS = 64
FRESH_ROWS = 32
BLOCK_ROWS = WEIGHT_ROWS + QUERY_ROWS + FRESH_ROWS
TURN_ROWS = TURN_TOKENS // TP
KEYS = PREFIX_PAGE_CAP * PAGE_POSITIONS
GROUP_ROWS = 512
CHUNKS = 4
CHUNK = 1024
VMEM_LIMIT = 56 * 1024 * 1024

MESH = pl.DeviceIdType.MESH
NT = (((1,), (1,)), ((), ()))
TN = (((0,), (0,)), ((), ()))


def remote(src, dst, send_sem, recv_sem, **axes):
    return pltpu.make_async_remote_copy(
        src_ref=src,
        dst_ref=dst,
        send_sem=send_sem,
        recv_sem=recv_sem,
        device_id=axes,
        device_id_type=MESH,
    )


def wait_bytes(like, sem):
    pltpu.make_async_copy(like, like, sem).wait()


def half_columns(keys, values, parity):
    low = lax.broadcasted_iota(jnp.int32, keys.shape, 1) < 64
    even = jnp.where(low, keys, pltpu.roll(values, 64, 1))
    odd = jnp.where(low, pltpu.roll(keys, 64, 1), values)
    return jnp.where(parity == 0, even, odd).astype(jnp.bfloat16)


def iota(shape, dimension):
    return lax.broadcasted_iota(jnp.int32, shape, dimension)


def one_hot(condition):
    return jnp.where(condition, 1.0, 0.0).astype(jnp.bfloat16)


def layer_kernel(
    prefix_pages,
    row_request,
    holder_table,
    store,
    turn,
    weight,
    step_query,
    fresh_rows_in,
    query,
    out,
    decode_out,
    pages_in,
    turn_in,
    gathered,
    rows_to_ring,
    fetched,
    by_head,
    turn_by_head,
    cache_kv,
    turn_kv,
    pages_out,
    turn_out,
    page_pick,
    live_bias,
    attention,
    decoded,
    from_pool,
    partial,
    from_x,
    mid,
    from_y,
    fetch_send,
    fetch_recv,
    head_send,
    head_recv,
    turn_head_send,
    turn_head_recv,
    page_send,
    page_recv,
    turn_send,
    turn_recv,
    ring_send,
    ring_recv,
    pair_send,
    pair_recv,
    core_send,
    core_recv,
    own_sem,
    pool_send,
    pool_recv,
    x_send,
    x_recv,
    y_send,
    y_recv,
):
    me = lax.axis_index("pool")
    rank = lax.axis_index("tp")
    z = me // 4
    y_hi = (me // 2) % 2
    core = me % 2
    x = rank // 4
    y = rank % 4
    other_core = me + 1 - 2 * core
    partner = me + 2 - 4 * y_hi

    barrier = pltpu.get_barrier_semaphore()

    def greet_pool(i, carry):
        pl.semaphore_signal(
            barrier, inc=1, device_id={"pool": (me + i) % POOL}, device_id_type=MESH
        )
        return carry

    def greet_tp(i, carry):
        pl.semaphore_signal(
            barrier, inc=1, device_id={"tp": (rank + i) % TP}, device_id_type=MESH
        )
        return carry

    lax.fori_loop(1, POOL, greet_pool, 0)
    lax.fori_loop(1, TP, greet_tp, 0)

    def place(at_z, at_y):
        return ((at_z + 8) % 8) * 2 + at_y

    own_place = place(z, y_hi)
    pair_place = place(z, 1 - y_hi)
    own_block = gathered.at[core, own_place]
    weight_copy = pltpu.make_async_copy(
        weight, own_block.at[pl.ds(0, WEIGHT_ROWS)], own_sem.at[0]
    )
    rows_copy = pltpu.make_async_copy(
        rows_to_ring, own_block.at[pl.ds(WEIGHT_ROWS, QUERY_ROWS + FRESH_ROWS)], own_sem.at[1]
    )
    weight_copy.start()
    for step in range(DECODE_STEPS):
        for pair in range(HEADS_DEV // 2):
            both = [
                step_query[step, :, head * HEAD_SIZE : (head + 1) * HEAD_SIZE]
                for head in (2 * pair, 2 * pair + 1)
            ]
            rows_to_ring[pl.ds(step * 32 + pair * 16, 16), :] = jnp.concatenate(both, axis=0)
    rows_to_ring[pl.ds(QUERY_ROWS, FRESH_ROWS), :] = fresh_rows_in[...]
    rows_copy.start()

    slots = (me + POOL - holder_table[pl.ds(me, 1), :]) % POOL
    wide = (128, PREFIX_PAGE_CAP)
    slot_live = jnp.max(
        jnp.where((slots == iota(wide, 0) // 4) & (iota(wide, 1) < prefix_pages[me]), 1.0, 0.0),
        axis=1,
        keepdims=True,
    )
    live_bias[...] = jnp.broadcast_to(
        jnp.where(slot_live > 0.0, 0.0, -jnp.inf), live_bias.shape
    )
    tall = (512, PREFIX_PAGE_CAP)
    wanted_page = (iota(tall, 0) // 16 + POOL - me) % POOL
    row_slot = jnp.sum(
        jnp.where(iota(tall, 1) == wanted_page, slots, 0), axis=1, keepdims=True
    )
    row_code = row_slot * 16 + iota((512, 1), 0) % 16
    lane = iota((1, 512), 1)
    lane_code = ((lane % 128) // 4) * 16 + (lane // 128) * 4 + lane % 4
    page_pick[...] = one_hot(row_code == lane_code)
    for kv in range(2):
        for head in range(KEY_VALUE_HEADS):
            turn_by_head[head, kv] = turn[kv, :, head * HEAD_SIZE : (head + 1) * HEAD_SIZE]
    weight_copy.wait()
    rows_copy.wait()

    pl.semaphore_wait(barrier, POOL - 1 + TP - 1)

    def fetch_copy(i):
        to = (me + i) % POOL
        return remote(
            store.at[to], fetched.at[i], fetch_send, fetch_recv.at[i // 4], pool=to
        )

    def start_fetch(i, carry):
        fetch_copy(i).start()
        return carry

    lax.fori_loop(1, POOL, start_fetch, 0)

    def ring_copy(direction, step, at_y):
        sign = 1 - 2 * direction
        slot = gathered.at[core, place(z - sign * step, at_y)]
        to = ((z + sign + 8) % 8) * 4 + y_hi * 2 + core
        return remote(slot, slot, ring_send, ring_recv.at[direction, step, at_y], pool=to)

    def core_copy(at):
        slot = gathered.at[core, at]
        return remote(slot, slot, core_send, core_recv, pool=other_core)

    def arrived(direction, step, at_y):
        sign = 1 - 2 * direction
        return place(z - sign * (step + 1), at_y)

    pair_copy = remote(own_block, own_block, pair_send, pair_recv, pool=partner)
    pair_copy.start()
    for direction in range(2):
        ring_copy(direction, 0, y_hi).start()

    def turn_head_copy(i):
        to = (rank + i) % TP
        return remote(
            turn_by_head.at[to // 2], turn_kv.at[rank], turn_head_send, turn_head_recv, tp=to
        )

    def start_turn_head(i, carry):
        turn_head_copy(i).start()
        return carry

    lax.fori_loop(1, TP, start_turn_head, 0)
    core_copy(own_place).start()
    fetched[0] = store[me]
    turn_kv[rank] = turn_by_head[rank // 2]

    def head_copy(i, part):
        to = (rank + i) % TP
        rows = pl.ds(part * 64, 64)
        return remote(
            by_head.at[to // 2, :, rows], cache_kv.at[rank, :, rows], head_send, head_recv, tp=to
        )

    def forward_pair():
        pair_copy.wait_recv()
        for direction in range(2):
            ring_copy(direction, 0, 1 - y_hi).start()
        core_copy(pair_place).start()

    def ring_step(step):
        for at_y in range(2):
            for direction in range(2):
                ring_copy(direction, step - 1, at_y).wait_recv()
                if step < 3 or at_y == direction:
                    ring_copy(direction, step, at_y).start()
                core_copy(arrived(direction, step - 1, at_y)).start()

    for part in range(2):

        def one_group(group, carry):
            for kv in range(2):
                rows = fetched[pl.ds(group * 4, 4), kv].astype(jnp.float32)
                rows = rows.reshape(16, KEY_VALUE_HEADS * HEAD_SIZE).astype(jnp.bfloat16)
                for head in range(KEY_VALUE_HEADS):
                    by_head[head, kv, pl.ds(group * 16, 16), :] = rows[
                        :, head * HEAD_SIZE : (head + 1) * HEAD_SIZE
                    ]
            return carry

        def wait_group(group, carry):
            wait_bytes(fetched.at[pl.ds(group * 4, 4)], fetch_recv.at[group])
            return one_group(group, carry)

        if part == 0:
            wait_bytes(fetched.at[pl.ds(1, 3)], fetch_recv.at[0])
            one_group(0, 0)
            lax.fori_loop(1, 4, wait_group, 0)
        else:
            lax.fori_loop(4, 8, wait_group, 0)

        def start_head(i, carry):
            head_copy(i, part).start()
            return carry

        lax.fori_loop(1, TP, start_head, 0)
        if part == 0:
            forward_pair()
    cache_kv[rank] = by_head[rank // 2]
    ring_step(1)
    ring_step(2)
    ring_step(3)
    wait_bytes(cache_kv.at[pl.ds(0, TP - 1)], head_recv)
    wait_bytes(turn_kv.at[pl.ds(0, TP - 1)], turn_head_recv)

    parity = rank % 2

    def page_group(group, carry):
        members = pl.ds(group * 4, 4)
        rows = [
            cache_kv[members, kv].reshape(512, HEAD_SIZE).astype(jnp.float32) for kv in range(2)
        ]
        halves = half_columns(rows[0], rows[1], parity)
        picked = jnp.dot(page_pick[...], halves, preferred_element_type=jnp.float32)
        pages_out[:, pl.ds(group * 16, 16), :] = picked.astype(jnp.bfloat16).reshape(
            POOL, 16, HEAD_SIZE
        )
        rows = [
            turn_kv[members, kv].reshape(64, HEAD_SIZE).astype(jnp.float32) for kv in range(2)
        ]
        turn_out[group] = half_columns(rows[0], rows[1], parity)
        return carry

    lax.fori_loop(0, 4, page_group, 0)

    def start_page(i, carry):
        to = (me + i) % POOL
        remote(pages_out.at[to], pages_in.at[i], page_send, page_recv, pool=to).start()
        return carry

    def start_turn(i, carry):
        remote(
            turn_out.at[i], turn_in.at[i], turn_send, turn_recv, pool=(me + i) % POOL
        ).start()
        return carry

    lax.fori_loop(1, POOL, start_page, 0)
    lax.fori_loop(1, 4, start_turn, 0)
    pages_in[0] = pages_out[me]
    turn_in[0] = turn_out[0]

    def attend(rows, turn_mask, fresh):
        scores = lax.dot_general(
            cache_kv[:, 0].reshape(KEYS, HEAD_SIZE),
            rows,
            NT,
            preferred_element_type=jnp.float32,
        )
        bias = jnp.concatenate([live_bias[...]] * (GROUP_ROWS // 128), axis=1)
        scores = (scores.reshape(TP, 128, GROUP_ROWS) + bias[None]).reshape(KEYS, GROUP_ROWS)
        turn_scores = lax.dot_general(
            turn_kv[:, 0].reshape(TURN_TOKENS, HEAD_SIZE),
            rows,
            NT,
            preferred_element_type=jnp.float32,
        )
        if turn_mask is not None:
            turn_scores = jnp.where(turn_mask, turn_scores, -jnp.inf)
        top = jnp.maximum(
            jnp.max(scores, axis=0, keepdims=True), jnp.max(turn_scores, axis=0, keepdims=True)
        )
        for score, _ in fresh:
            top = jnp.maximum(top, score)
        top = top * EXP2_SCALE
        exponent = jnp.exp2(scores * EXP2_SCALE - top)
        turn_exponent = jnp.exp2(turn_scores * EXP2_SCALE - top)
        total = jnp.sum(exponent, axis=0, keepdims=True) + jnp.sum(
            turn_exponent, axis=0, keepdims=True
        )
        mixed = lax.dot_general(
            cache_kv[:, 1].reshape(KEYS, HEAD_SIZE),
            exponent.astype(jnp.bfloat16),
            TN,
            preferred_element_type=jnp.float32,
        ) + lax.dot_general(
            turn_kv[:, 1].reshape(TURN_TOKENS, HEAD_SIZE),
            turn_exponent.astype(jnp.bfloat16),
            TN,
            preferred_element_type=jnp.float32,
        )
        for score, value in fresh:
            share = jnp.exp2(score * EXP2_SCALE - top)
            total = total + share
            mixed = mixed + share * value
        return (mixed / total).T.astype(jnp.bfloat16)

    def attend_rows(half):
        causal = (TURN_TOKENS, GROUP_ROWS)
        at = iota(causal, 1) % 128
        mask = iota(causal, 0) <= (at // 32) * 64 + half * 32 + at % 32
        heads = [slice(head * HEAD_SIZE, (head + 1) * HEAD_SIZE) for head in range(HEADS_DEV)]
        rows = [query[:, half, :, columns].reshape(128, HEAD_SIZE) for columns in heads]
        result = attend(jnp.concatenate(rows, axis=0), mask, ())
        for head, columns in enumerate(heads):
            attention[:, columns] = result[head * 128 : (head + 1) * 128]

    def send_x(half, chunk, to):
        @pl.when(to != x)
        def _():
            slot = (to - x + 4) % 4
            remote(
                partial.at[half, chunk, to],
                from_x.at[half, chunk, slot],
                x_send,
                x_recv.at[half, chunk],
                tp=to * 4 + y,
            ).start()

    def project(half):
        def one_chunk(chunk, carry):
            def one_place(i, inner):
                both = [gathered[k, chunk * 4 + i, :WEIGHT_ROWS] for k in range(2)]
                product = jnp.dot(
                    attention[...],
                    jnp.concatenate(both, axis=1),
                    preferred_element_type=jnp.float32,
                )
                columns = pl.ds(pl.multiple_of(i * 256, 256), 256)
                partial[half, chunk, :, :, columns] = product.astype(jnp.bfloat16).reshape(
                    4, 32, 256
                )
                return inner

            lax.fori_loop(0, 4, one_place, 0)
            for i in (2, 1, 3):
                send_x(half, chunk, (x + i) % 4)
            return carry

        lax.fori_loop(0, CHUNKS, one_chunk, 0)

    for direction in range(2):
        ring_copy(direction, 3, direction).wait_recv()
        core_copy(arrived(direction, 3, direction)).start()
    attend_rows(0)
    wait_bytes(gathered.at[1 - core], core_recv)
    project(0)
    attend_rows(1)
    project(1)

    def decode_block(b):
        part_core = b // 2
        places = pl.ds((b % 2) * 8, 8)
        rows = gathered[part_core, places, WEIGHT_ROWS : WEIGHT_ROWS + QUERY_ROWS].reshape(
            GROUP_ROWS, HEAD_SIZE
        )
        fresh_rows = (
            gathered[part_core, places, WEIGHT_ROWS + QUERY_ROWS :]
            .astype(jnp.float32)
            .reshape(8, 4, 1, 8, HEAD_SIZE)
        )
        rows_wide = rows.astype(jnp.float32)
        fresh = []
        for step in range(DECODE_STEPS):
            key, value = (
                jnp.broadcast_to(fresh_rows[:, 2 * step + kv], (8, 8, 8, HEAD_SIZE)).reshape(
                    GROUP_ROWS, HEAD_SIZE
                )
                for kv in range(2)
            )
            score = jnp.sum((rows_wide * key).T, axis=0, keepdims=True)
            if step == 1:
                score = jnp.where(iota((1, GROUP_ROWS), 1) % 64 >= 32, score, -jnp.inf)
            fresh.append((score, value.T))
        result = attend(rows, None, fresh).reshape(8, QUERY_ROWS, HEAD_SIZE)
        for k in range(8):
            to = ((b % 2) * 8 + k) * 2 + part_core
            slot = (to - me + POOL) % POOL
            decoded[slot] = result[k]

            @pl.when(slot > 0)
            def _():
                remote(
                    decoded.at[slot], from_pool.at[slot], pool_send, pool_recv, pool=to
                ).start()

    def add_x(half, chunk):
        wait_bytes(from_x.at[half, chunk, pl.ds(1, 3)], x_recv.at[half, chunk])
        rows = partial[half, chunk, x].astype(jnp.float32)
        for i in range(1, 4):
            rows = rows + from_x[half, chunk, i].astype(jnp.float32)
        mid[half, chunk] = rows.astype(jnp.bfloat16)
        for k in range(2):
            to = half * 2 + k

            @pl.when(to != y)
            def _():
                remote(
                    mid.at[half, chunk, pl.ds(k * 16, 16)],
                    from_y.at[chunk, (to - y + 4) % 4],
                    y_send.at[half, k],
                    y_recv.at[chunk],
                    tp=x * 4 + to,
                ).start()

    def decode_and_add(i, carry):
        decode_block(i)
        add_x(i // 2, (i % 2) * 2)
        add_x(i // 2, (i % 2) * 2 + 1)
        return carry

    lax.fori_loop(0, 4, decode_and_add, 0)

    wait_bytes(from_pool.at[pl.ds(1, POOL - 1)], pool_recv)
    row_at = iota((QUERY_ROWS, HEAD_SIZE), 0) % 8
    groups = jnp.zeros((QUERY_ROWS, HEAD_SIZE), jnp.int32)
    for k in range(8):
        groups = jnp.where(row_at == k, row_request[me * 8 + k], groups)

    def add_pool(i, carry):
        return jnp.where(
            groups == (me + POOL - i) % POOL, from_pool[i].astype(jnp.float32), carry
        )

    own = decoded[0].astype(jnp.float32)
    decode_out[...] = lax.fori_loop(1, POOL, add_pool, own).astype(jnp.bfloat16)

    def add_y(chunk, carry):
        wait_bytes(from_y.at[chunk, pl.ds(1, 3)], y_recv.at[chunk])
        rows = mid[y // 2, chunk, pl.ds((y % 2) * 16, 16), :].astype(jnp.float32)
        for i in range(1, 4):
            rows = rows + from_y[chunk, i].astype(jnp.float32)
        out[:, pl.ds(pl.multiple_of(chunk * CHUNK, CHUNK), CHUNK)] = rows.astype(jnp.bfloat16)
        return carry

    lax.fori_loop(0, CHUNKS, add_y, 0)

    wait_bytes(pages_in.at[pl.ds(1, POOL - 1)], page_recv)
    wait_bytes(turn_in.at[pl.ds(1, 3)], turn_recv)
    wait_bytes(store.at[pl.ds(1, POOL - 1)], fetch_send)
    wait_bytes(cache_kv.at[pl.ds(0, TP - 1)], head_send)
    wait_bytes(turn_kv.at[pl.ds(0, TP - 1)], turn_head_send)
    wait_bytes(pages_out.at[pl.ds(1, POOL - 1)], page_send)
    wait_bytes(turn_out.at[pl.ds(1, 3)], turn_send)
    wait_bytes(gathered.at[0, pl.ds(0, 14)], ring_send)
    pair_copy.wait_send()
    wait_bytes(gathered.at[core], core_send)
    wait_bytes(decoded.at[pl.ds(1, POOL - 1)], pool_send)
    wait_bytes(from_x.at[:, :, pl.ds(1, 3)], x_send)
    for half in range(2):
        for k in range(2):

            @pl.when(half * 2 + k != y)
            def _():
                wait_bytes(from_y.at[:, 0], y_send.at[half, k])


def layer_call(*operands):
    vmem = pl.BlockSpec(memory_space=pltpu.VMEM)
    smem = pl.BlockSpec(memory_space=pltpu.SMEM)
    anywhere = pl.BlockSpec(memory_space=pl.ANY)
    dma = pltpu.SemaphoreType.DMA
    scratch = [
        (2, 16, BLOCK_ROWS, HEAD_SIZE),
        (QUERY_ROWS + FRESH_ROWS, HEAD_SIZE),
        (POOL, 2, 4, KEY_VALUE_HEADS * HEAD_SIZE),
        (KEY_VALUE_HEADS, 2, 128, HEAD_SIZE),
        (KEY_VALUE_HEADS, 2, TURN_ROWS, HEAD_SIZE),
        (TP, 2, 128, HEAD_SIZE),
        (TP, 2, TURN_ROWS, HEAD_SIZE),
        (POOL, PAGE_POSITIONS, HEAD_SIZE),
        (4, PAGE_POSITIONS, HEAD_SIZE),
        (512, 512),
        (128, 128),
        (TURN_TOKENS // 2, HEADS_DEV * HEAD_SIZE),
        (POOL, QUERY_ROWS, HEAD_SIZE),
        (POOL, QUERY_ROWS, HEAD_SIZE),
        (2, CHUNKS, 4, 32, CHUNK),
        (2, CHUNKS, 4, 32, CHUNK),
        (2, CHUNKS, 32, CHUNK),
        (CHUNKS, 4, 16, CHUNK),
    ]
    return pl.pallas_call(
        layer_kernel,
        out_shape=(
            jax.ShapeDtypeStruct((16, CHUNKS * CHUNK), jnp.bfloat16),
            jax.ShapeDtypeStruct((QUERY_ROWS, HEAD_SIZE), jnp.bfloat16),
            jax.ShapeDtypeStruct((POOL, PAGE_POSITIONS, HEAD_SIZE), jnp.bfloat16),
            jax.ShapeDtypeStruct((4, PAGE_POSITIONS, HEAD_SIZE), jnp.bfloat16),
        ),
        in_specs=[smem, smem, vmem, vmem, vmem, anywhere, vmem, vmem, vmem],
        out_specs=(vmem, vmem, vmem, vmem),
        scratch_shapes=[
            pltpu.VMEM(shape, jnp.float32 if shape == (128, 128) else jnp.bfloat16)
            for shape in scratch
        ]
        + [
            dma,
            dma((8,)),
            dma,
            dma,
            dma,
            dma,
            dma,
            dma,
            dma,
            dma,
            dma,
            dma((2, 4, 2)),
            dma,
            dma,
            dma,
            dma,
            dma((2,)),
            dma,
            dma,
            dma,
            dma((2, CHUNKS)),
            dma((2, 2)),
            dma((CHUNKS,)),
        ],
        compiler_params=pltpu.CompilerParams(
            collective_id=0, has_side_effects=True, vmem_limit_bytes=VMEM_LIMIT
        ),
        name="attention_layer",
    )(*operands)


CACHE_STEP = 8


def last_kernel(pages_in, turn_in, prefill_in, decode_in, cache, prefill_out, decode_out):
    me = lax.axis_index("pool")
    first = pl.program_id(0) * CACHE_STEP

    @pl.when(first == 0)
    def _():
        prefill_out[...] = prefill_in[...]
        for step in range(DECODE_STEPS):
            for head in range(HEADS_DEV):
                rows = decode_in[step * 32 + head * 8 : step * 32 + head * 8 + 8]
                decode_out[step, :, head * HEAD_SIZE : (head + 1) * HEAD_SIZE] = rows

    for k in range(CACHE_STEP):
        slot = (me - first - k + 2 * POOL) % POOL
        page = pages_in[slot]
        turn_page = turn_in[jnp.minimum(slot, 3)]
        turn_page = jnp.where(slot < 4, turn_page, jnp.zeros_like(turn_page))
        for kv in range(2):
            columns = slice(kv * 64, kv * 64 + 64)
            cache[0, k, 0, kv] = page[:, columns]
            cache[0, k, 1, kv] = turn_page[:, columns]


def last_call(pages_in, turn_in, prefill, decoded):
    vmem = pl.BlockSpec(memory_space=pltpu.VMEM)
    tail = (2, 2, PAGE_POSITIONS, 64)
    decode_shape = (DECODE_STEPS, 8, HEADS_DEV * HEAD_SIZE)
    return pl.pallas_call(
        last_kernel,
        grid=(POOL // CACHE_STEP,),
        out_shape=(
            jax.ShapeDtypeStruct((1, POOL) + tail, jnp.bfloat16),
            jax.ShapeDtypeStruct(prefill.shape, jnp.bfloat16),
            jax.ShapeDtypeStruct(decode_shape, jnp.bfloat16),
        ),
        in_specs=[vmem] * 4,
        out_specs=(
            pl.BlockSpec((1, CACHE_STEP) + tail, lambda i: (0, i, 0, 0, 0, 0)),
            pl.BlockSpec(prefill.shape, lambda i: (0, 0)),
            pl.BlockSpec(decode_shape, lambda i: (0, 0, 0)),
        ),
        compiler_params=pltpu.CompilerParams(vmem_limit_bytes=VMEM_LIMIT),
        name="lay_out_results",
    )(pages_in, turn_in, prefill, decoded)


def per_device(
    turn_query_rows,
    turn_key_value,
    prefix_page_store,
    prefix_pages,
    holder_table,
    out_weight,
    row_request,
    step_query,
    step_kv,
):
    rank = lax.axis_index("tp")
    fresh = lax.dynamic_slice_in_dim(step_kv, (rank // 2) * HEAD_SIZE, HEAD_SIZE, 3)
    fresh = jnp.transpose(fresh, (0, 2, 1, 3)).reshape(FRESH_ROWS, HEAD_SIZE)
    prefill_out, decode_rows, pages_in, turn_in = layer_call(
        prefix_pages,
        row_request,
        holder_table,
        prefix_page_store,
        turn_key_value.reshape(2, TURN_ROWS, KEY_VALUE_HEADS * HEAD_SIZE),
        out_weight,
        step_query,
        fresh,
        turn_query_rows.reshape(4, 2, 32, HEADS_DEV * HEAD_SIZE),
    )
    decode_cache, prefill_out, decode_out = last_call(
        pages_in, turn_in, prefill_out, decode_rows
    )
    return (prefill_out, decode_out, decode_cache)


def solution(mesh):
    placed = (
        P("pool", "tp"),
        P("pool", None, "tp", None),
        P("pool", None, "tp", None),
        P(),
        P(),
        P("tp", "pool"),
        P(),
        P(None, "pool", "tp"),
        P(None, "pool", None, None),
    )
    return jax.shard_map(
        per_device,
        mesh=mesh,
        in_specs=placed,
        out_specs=(
            P(("pool", "tp"), None),
            P(None, "pool", "tp"),
            P("pool", None, None, None, None, "tp"),
        ),
        check_vma=False,
    )
```

```python
import math

import jax
import jax.numpy as jnp
from jax import lax
from jax.experimental import pallas as pl
from jax.experimental.pallas import tpu as pltpu
from jax.sharding import PartitionSpec as P

QUERY_HEADS = 64
KEY_VALUE_HEADS = 8
HEAD_SIZE = 128
PAGE_POSITIONS = 64
PREFIX_PAGE_CAP = 32
TURN_TOKENS = 256
DECODE_STEPS = 2
POOL = 32
TP = 16
HEADS_DEV = QUERY_HEADS // TP
SCORE_SCALE = 1.0 / math.sqrt(HEAD_SIZE)
EXP2_SCALE = SCORE_SCALE * math.log2(math.e)
WEIGHT_ROWS = 512
QUERY_ROWS = 64
FRESH_ROWS = 32
BLOCK_ROWS = WEIGHT_ROWS + QUERY_ROWS + FRESH_ROWS
TURN_ROWS = TURN_TOKENS // TP
KEYS = PREFIX_PAGE_CAP * PAGE_POSITIONS
GROUP_ROWS = 512
CHUNKS = 4
CHUNK = 1024
VMEM_LIMIT = 56 * 1024 * 1024

MESH = pl.DeviceIdType.MESH
NT = (((1,), (1,)), ((), ()))
TN = (((0,), (0,)), ((), ()))


def remote(src, dst, send_sem, recv_sem, **axes):
    return pltpu.make_async_remote_copy(
        src_ref=src,
        dst_ref=dst,
        send_sem=send_sem,
        recv_sem=recv_sem,
        device_id=axes,
        device_id_type=MESH,
    )


def wait_bytes(like, sem):
    pltpu.make_async_copy(like, like, sem).wait()


def half_columns(keys, values, parity):
    low = lax.broadcasted_iota(jnp.int32, keys.shape, 1) < 64
    even = jnp.where(low, keys, pltpu.roll(values, 64, 1))
    odd = jnp.where(low, pltpu.roll(keys, 64, 1), values)
    return jnp.where(parity == 0, even, odd).astype(jnp.bfloat16)


def iota(shape, dimension):
    return lax.broadcasted_iota(jnp.int32, shape, dimension)


def one_hot(condition):
    return jnp.where(condition, 1.0, 0.0).astype(jnp.bfloat16)


def layer_kernel(
    prefix_pages,
    row_request,
    holder_table,
    store,
    turn,
    weight,
    step_query,
    fresh_rows_in,
    query,
    out,
    decode_out,
    pages_in,
    turn_in,
    gathered,
    rows_to_ring,
    fetched,
    by_head,
    turn_by_head,
    cache_kv,
    turn_kv,
    pages_out,
    turn_out,
    page_pick,
    live_bias,
    attention,
    decoded,
    from_pool,
    partial,
    from_x,
    mid,
    from_y,
    fetch_send,
    fetch_recv,
    head_send,
    head_recv,
    turn_head_send,
    turn_head_recv,
    page_send,
    page_recv,
    turn_send,
    turn_recv,
    ring_send,
    ring_recv,
    pair_send,
    pair_recv,
    core_send,
    core_recv,
    own_sem,
    pool_send,
    pool_recv,
    x_send,
    x_recv,
    y_send,
    y_recv,
):
    me = lax.axis_index("pool")
    rank = lax.axis_index("tp")
    z = me // 4
    y_hi = (me // 2) % 2
    core = me % 2
    x = rank // 4
    y = rank % 4
    other_core = me + 1 - 2 * core
    partner = me + 2 - 4 * y_hi

    barrier = pltpu.get_barrier_semaphore()

    def greet_pool(i, carry):
        pl.semaphore_signal(
            barrier, inc=1, device_id={"pool": (me + i) % POOL}, device_id_type=MESH
        )
        return carry

    def greet_tp(i, carry):
        pl.semaphore_signal(
            barrier, inc=1, device_id={"tp": (rank + i) % TP}, device_id_type=MESH
        )
        return carry

    lax.fori_loop(1, POOL, greet_pool, 0)
    lax.fori_loop(1, TP, greet_tp, 0)

    def place(at_z, at_y):
        return ((at_z + 8) % 8) * 2 + at_y

    own_place = place(z, y_hi)
    pair_place = place(z, 1 - y_hi)
    own_block = gathered.at[core, own_place]
    weight_copy = pltpu.make_async_copy(
        weight, own_block.at[pl.ds(0, WEIGHT_ROWS)], own_sem.at[0]
    )
    rows_copy = pltpu.make_async_copy(
        rows_to_ring, own_block.at[pl.ds(WEIGHT_ROWS, QUERY_ROWS + FRESH_ROWS)], own_sem.at[1]
    )
    weight_copy.start()
    for step in range(DECODE_STEPS):
        for pair in range(HEADS_DEV // 2):
            both = [
                step_query[step, :, head * HEAD_SIZE : (head + 1) * HEAD_SIZE]
                for head in (2 * pair, 2 * pair + 1)
            ]
            rows_to_ring[pl.ds(step * 32 + pair * 16, 16), :] = jnp.concatenate(both, axis=0)
    rows_to_ring[pl.ds(QUERY_ROWS, FRESH_ROWS), :] = fresh_rows_in[...]
    rows_copy.start()

    slots = (me + POOL - holder_table[pl.ds(me, 1), :]) % POOL
    wide = (128, PREFIX_PAGE_CAP)
    slot_live = jnp.max(
        jnp.where((slots == iota(wide, 0) // 4) & (iota(wide, 1) < prefix_pages[me]), 1.0, 0.0),
        axis=1,
        keepdims=True,
    )
    live_bias[...] = jnp.broadcast_to(
        jnp.where(slot_live > 0.0, 0.0, -jnp.inf), live_bias.shape
    )
    tall = (512, PREFIX_PAGE_CAP)
    wanted_page = (iota(tall, 0) // 16 + POOL - me) % POOL
    row_slot = jnp.sum(
        jnp.where(iota(tall, 1) == wanted_page, slots, 0), axis=1, keepdims=True
    )
    row_code = row_slot * 16 + iota((512, 1), 0) % 16
    lane = iota((1, 512), 1)
    lane_code = ((lane % 128) // 4) * 16 + (lane // 128) * 4 + lane % 4
    page_pick[...] = one_hot(row_code == lane_code)
    for kv in range(2):
        for head in range(KEY_VALUE_HEADS):
            turn_by_head[head, kv] = turn[kv, :, head * HEAD_SIZE : (head + 1) * HEAD_SIZE]
    weight_copy.wait()
    rows_copy.wait()

    pl.semaphore_wait(barrier, POOL - 1 + TP - 1)

    def fetch_copy(i):
        to = (me + i) % POOL
        return remote(
            store.at[to], fetched.at[i], fetch_send, fetch_recv.at[i // 4], pool=to
        )

    def start_fetch(i, carry):
        fetch_copy(i).start()
        return carry

    lax.fori_loop(1, POOL, start_fetch, 0)

    def ring_copy(direction, step, at_y):
        sign = 1 - 2 * direction
        slot = gathered.at[core, place(z - sign * step, at_y)]
        to = ((z + sign + 8) % 8) * 4 + y_hi * 2 + core
        return remote(slot, slot, ring_send, ring_recv.at[direction, step, at_y], pool=to)

    def core_copy(at):
        slot = gathered.at[core, at]
        return remote(slot, slot, core_send, core_recv, pool=other_core)

    def arrived(direction, step, at_y):
        sign = 1 - 2 * direction
        return place(z - sign * (step + 1), at_y)

    pair_copy = remote(own_block, own_block, pair_send, pair_recv, pool=partner)
    pair_copy.start()
    for direction in range(2):
        ring_copy(direction, 0, y_hi).start()

    def turn_head_copy(i):
        to = (rank + i) % TP
        return remote(
            turn_by_head.at[to // 2], turn_kv.at[rank], turn_head_send, turn_head_recv, tp=to
        )

    def start_turn_head(i, carry):
        turn_head_copy(i).start()
        return carry

    lax.fori_loop(1, TP, start_turn_head, 0)
    core_copy(own_place).start()
    fetched[0] = store[me]
    turn_kv[rank] = turn_by_head[rank // 2]

    def head_copy(i, part):
        to = (rank + i) % TP
        rows = pl.ds(part * 64, 64)
        return remote(
            by_head.at[to // 2, :, rows], cache_kv.at[rank, :, rows], head_send, head_recv, tp=to
        )

    def forward_pair():
        pair_copy.wait_recv()
        for direction in range(2):
            ring_copy(direction, 0, 1 - y_hi).start()
        core_copy(pair_place).start()

    def ring_step(step, at_y):
        for direction in range(2):
            ring_copy(direction, step - 1, at_y).wait_recv()
            if step < 3:
                ring_copy(direction, step, at_y).start()
            else:

                @pl.when(at_y == direction)
                def _():
                    ring_copy(direction, step, at_y).start()

            core_copy(arrived(direction, step - 1, at_y)).start()

    for part in range(2):

        def one_group(group, carry):
            for kv in range(2):
                rows = fetched[pl.ds(group * 4, 4), kv].astype(jnp.float32)
                rows = rows.reshape(16, KEY_VALUE_HEADS * HEAD_SIZE).astype(jnp.bfloat16)
                for head in range(KEY_VALUE_HEADS):
                    by_head[head, kv, pl.ds(group * 16, 16), :] = rows[
                        :, head * HEAD_SIZE : (head + 1) * HEAD_SIZE
                    ]
            return carry

        def wait_group(group, carry):
            wait_bytes(fetched.at[pl.ds(group * 4, 4)], fetch_recv.at[group])
            return one_group(group, carry)

        if part == 0:
            wait_bytes(fetched.at[pl.ds(1, 3)], fetch_recv.at[0])
            one_group(0, 0)
            lax.fori_loop(1, 4, wait_group, 0)
        else:
            lax.fori_loop(4, 8, wait_group, 0)

        def start_head(i, carry):
            head_copy(i, part).start()
            return carry

        lax.fori_loop(1, TP, start_head, 0)
        if part == 0:
            ring_step(1, y_hi)
            forward_pair()
    cache_kv[rank] = by_head[rank // 2]
    ring_step(2, y_hi)
    ring_step(1, 1 - y_hi)
    ring_step(3, y_hi)
    ring_step(2, 1 - y_hi)
    ring_step(3, 1 - y_hi)
    wait_bytes(cache_kv.at[pl.ds(0, TP - 1)], head_recv)
    wait_bytes(turn_kv.at[pl.ds(0, TP - 1)], turn_head_recv)

    parity = rank % 2

    def page_group(group, carry):
        members = pl.ds(group * 4, 4)
        rows = [
            cache_kv[members, kv].reshape(512, HEAD_SIZE).astype(jnp.float32) for kv in range(2)
        ]
        halves = half_columns(rows[0], rows[1], parity)
        picked = jnp.dot(page_pick[...], halves, preferred_element_type=jnp.float32)
        pages_out[:, pl.ds(group * 16, 16), :] = picked.astype(jnp.bfloat16).reshape(
            POOL, 16, HEAD_SIZE
        )
        rows = [
            turn_kv[members, kv].reshape(64, HEAD_SIZE).astype(jnp.float32) for kv in range(2)
        ]
        turn_out[group] = half_columns(rows[0], rows[1], parity)
        return carry

    lax.fori_loop(0, 4, page_group, 0)

    def start_page(i, carry):
        to = (me + i) % POOL
        remote(pages_out.at[to], pages_in.at[i], page_send, page_recv, pool=to).start()
        return carry

    def start_turn(i, carry):
        remote(
            turn_out.at[i], turn_in.at[i], turn_send, turn_recv, pool=(me + i) % POOL
        ).start()
        return carry

    lax.fori_loop(1, POOL, start_page, 0)
    lax.fori_loop(1, 4, start_turn, 0)
    pages_in[0] = pages_out[me]
    turn_in[0] = turn_out[0]

    def attend(rows, turn_mask, fresh):
        scores = lax.dot_general(
            cache_kv[:, 0].reshape(KEYS, HEAD_SIZE),
            rows,
            NT,
            preferred_element_type=jnp.float32,
        )
        bias = jnp.concatenate([live_bias[...]] * (GROUP_ROWS // 128), axis=1)
        scores = (scores.reshape(TP, 128, GROUP_ROWS) + bias[None]).reshape(KEYS, GROUP_ROWS)
        turn_scores = lax.dot_general(
            turn_kv[:, 0].reshape(TURN_TOKENS, HEAD_SIZE),
            rows,
            NT,
            preferred_element_type=jnp.float32,
        )
        if turn_mask is not None:
            turn_scores = jnp.where(turn_mask, turn_scores, -jnp.inf)
        top = jnp.maximum(
            jnp.max(scores, axis=0, keepdims=True), jnp.max(turn_scores, axis=0, keepdims=True)
        )
        for score, _ in fresh:
            top = jnp.maximum(top, score)
        top = top * EXP2_SCALE
        exponent = jnp.exp2(scores * EXP2_SCALE - top)
        turn_exponent = jnp.exp2(turn_scores * EXP2_SCALE - top)
        total = jnp.sum(exponent, axis=0, keepdims=True) + jnp.sum(
            turn_exponent, axis=0, keepdims=True
        )
        mixed = lax.dot_general(
            cache_kv[:, 1].reshape(KEYS, HEAD_SIZE),
            exponent.astype(jnp.bfloat16),
            TN,
            preferred_element_type=jnp.float32,
        ) + lax.dot_general(
            turn_kv[:, 1].reshape(TURN_TOKENS, HEAD_SIZE),
            turn_exponent.astype(jnp.bfloat16),
            TN,
            preferred_element_type=jnp.float32,
        )
        for score, value in fresh:
            share = jnp.exp2(score * EXP2_SCALE - top)
            total = total + share
            mixed = mixed + share * value
        return (mixed / total).T.astype(jnp.bfloat16)

    def attend_rows(half):
        causal = (TURN_TOKENS, GROUP_ROWS)
        at = iota(causal, 1) % 128
        mask = iota(causal, 0) <= (at // 32) * 64 + half * 32 + at % 32
        heads = [slice(head * HEAD_SIZE, (head + 1) * HEAD_SIZE) for head in range(HEADS_DEV)]
        rows = [query[:, half, :, columns].reshape(128, HEAD_SIZE) for columns in heads]
        result = attend(jnp.concatenate(rows, axis=0), mask, ())
        for head, columns in enumerate(heads):
            attention[:, columns] = result[head * 128 : (head + 1) * 128]

    def send_x(half, chunk, to):
        @pl.when(to != x)
        def _():
            slot = (to - x + 4) % 4
            remote(
                partial.at[half, chunk, to],
                from_x.at[half, chunk, slot],
                x_send,
                x_recv.at[half, chunk],
                tp=to * 4 + y,
            ).start()

    def project(half):
        def one_chunk(chunk, carry):
            def one_place(i, inner):
                both = [gathered[k, chunk * 4 + i, :WEIGHT_ROWS] for k in range(2)]
                product = jnp.dot(
                    attention[...],
                    jnp.concatenate(both, axis=1),
                    preferred_element_type=jnp.float32,
                )
                columns = pl.ds(pl.multiple_of(i * 256, 256), 256)
                partial[half, chunk, :, :, columns] = product.astype(jnp.bfloat16).reshape(
                    4, 32, 256
                )
                return inner

            lax.fori_loop(0, 4, one_place, 0)
            for i in (2, 1, 3):
                send_x(half, chunk, (x + i) % 4)
            return carry

        lax.fori_loop(0, CHUNKS, one_chunk, 0)

    for direction in range(2):
        ring_copy(direction, 3, direction).wait_recv()
        core_copy(arrived(direction, 3, direction)).start()
    attend_rows(0)
    wait_bytes(gathered.at[1 - core], core_recv)
    project(0)
    attend_rows(1)
    project(1)

    def decode_block(b):
        part_core = b // 2
        places = pl.ds((b % 2) * 8, 8)
        rows = gathered[part_core, places, WEIGHT_ROWS : WEIGHT_ROWS + QUERY_ROWS].reshape(
            GROUP_ROWS, HEAD_SIZE
        )
        fresh_rows = (
            gathered[part_core, places, WEIGHT_ROWS + QUERY_ROWS :]
            .astype(jnp.float32)
            .reshape(8, 4, 1, 8, HEAD_SIZE)
        )
        rows_wide = rows.astype(jnp.float32)
        fresh = []
        for step in range(DECODE_STEPS):
            key, value = (
                jnp.broadcast_to(fresh_rows[:, 2 * step + kv], (8, 8, 8, HEAD_SIZE)).reshape(
                    GROUP_ROWS, HEAD_SIZE
                )
                for kv in range(2)
            )
            score = jnp.sum((rows_wide * key).T, axis=0, keepdims=True)
            if step == 1:
                score = jnp.where(iota((1, GROUP_ROWS), 1) % 64 >= 32, score, -jnp.inf)
            fresh.append((score, value.T))
        result = attend(rows, None, fresh).reshape(8, QUERY_ROWS, HEAD_SIZE)
        for k in range(8):
            to = ((b % 2) * 8 + k) * 2 + part_core
            slot = (to - me + POOL) % POOL
            decoded[slot] = result[k]

            @pl.when(slot > 0)
            def _():
                remote(
                    decoded.at[slot], from_pool.at[slot], pool_send, pool_recv, pool=to
                ).start()

    def add_x(half, chunk):
        wait_bytes(from_x.at[half, chunk, pl.ds(1, 3)], x_recv.at[half, chunk])
        rows = partial[half, chunk, x].astype(jnp.float32)
        for i in range(1, 4):
            rows = rows + from_x[half, chunk, i].astype(jnp.float32)
        mid[half, chunk] = rows.astype(jnp.bfloat16)
        for k in range(2):
            to = half * 2 + k

            @pl.when(to != y)
            def _():
                remote(
                    mid.at[half, chunk, pl.ds(k * 16, 16)],
                    from_y.at[chunk, (to - y + 4) % 4],
                    y_send.at[half, k],
                    y_recv.at[chunk],
                    tp=x * 4 + to,
                ).start()

    def decode_and_add(i, carry):
        decode_block(i)
        add_x(i // 2, (i % 2) * 2)
        add_x(i // 2, (i % 2) * 2 + 1)
        return carry

    lax.fori_loop(0, 4, decode_and_add, 0)

    wait_bytes(from_pool.at[pl.ds(1, POOL - 1)], pool_recv)
    row_at = iota((QUERY_ROWS, HEAD_SIZE), 0) % 8
    groups = jnp.zeros((QUERY_ROWS, HEAD_SIZE), jnp.int32)
    for k in range(8):
        groups = jnp.where(row_at == k, row_request[me * 8 + k], groups)

    def add_pool(i, carry):
        return jnp.where(
            groups == (me + POOL - i) % POOL, from_pool[i].astype(jnp.float32), carry
        )

    own = decoded[0].astype(jnp.float32)
    decode_out[...] = lax.fori_loop(1, POOL, add_pool, own).astype(jnp.bfloat16)

    def add_y(chunk, carry):
        wait_bytes(from_y.at[chunk, pl.ds(1, 3)], y_recv.at[chunk])
        rows = mid[y // 2, chunk, pl.ds((y % 2) * 16, 16), :].astype(jnp.float32)
        for i in range(1, 4):
            rows = rows + from_y[chunk, i].astype(jnp.float32)
        out[:, pl.ds(pl.multiple_of(chunk * CHUNK, CHUNK), CHUNK)] = rows.astype(jnp.bfloat16)
        return carry

    lax.fori_loop(0, CHUNKS, add_y, 0)

    wait_bytes(pages_in.at[pl.ds(1, POOL - 1)], page_recv)
    wait_bytes(turn_in.at[pl.ds(1, 3)], turn_recv)
    wait_bytes(store.at[pl.ds(1, POOL - 1)], fetch_send)
    wait_bytes(cache_kv.at[pl.ds(0, TP - 1)], head_send)
    wait_bytes(turn_kv.at[pl.ds(0, TP - 1)], turn_head_send)
    wait_bytes(pages_out.at[pl.ds(1, POOL - 1)], page_send)
    wait_bytes(turn_out.at[pl.ds(1, 3)], turn_send)
    wait_bytes(gathered.at[0, pl.ds(0, 14)], ring_send)
    pair_copy.wait_send()
    wait_bytes(gathered.at[core], core_send)
    wait_bytes(decoded.at[pl.ds(1, POOL - 1)], pool_send)
    wait_bytes(from_x.at[:, :, pl.ds(1, 3)], x_send)
    for half in range(2):
        for k in range(2):

            @pl.when(half * 2 + k != y)
            def _():
                wait_bytes(from_y.at[:, 0], y_send.at[half, k])


def layer_call(*operands):
    vmem = pl.BlockSpec(memory_space=pltpu.VMEM)
    smem = pl.BlockSpec(memory_space=pltpu.SMEM)
    anywhere = pl.BlockSpec(memory_space=pl.ANY)
    dma = pltpu.SemaphoreType.DMA
    scratch = [
        (2, 16, BLOCK_ROWS, HEAD_SIZE),
        (QUERY_ROWS + FRESH_ROWS, HEAD_SIZE),
        (POOL, 2, 4, KEY_VALUE_HEADS * HEAD_SIZE),
        (KEY_VALUE_HEADS, 2, 128, HEAD_SIZE),
        (KEY_VALUE_HEADS, 2, TURN_ROWS, HEAD_SIZE),
        (TP, 2, 128, HEAD_SIZE),
        (TP, 2, TURN_ROWS, HEAD_SIZE),
        (POOL, PAGE_POSITIONS, HEAD_SIZE),
        (4, PAGE_POSITIONS, HEAD_SIZE),
        (512, 512),
        (128, 128),
        (TURN_TOKENS // 2, HEADS_DEV * HEAD_SIZE),
        (POOL, QUERY_ROWS, HEAD_SIZE),
        (POOL, QUERY_ROWS, HEAD_SIZE),
        (2, CHUNKS, 4, 32, CHUNK),
        (2, CHUNKS, 4, 32, CHUNK),
        (2, CHUNKS, 32, CHUNK),
        (CHUNKS, 4, 16, CHUNK),
    ]
    return pl.pallas_call(
        layer_kernel,
        out_shape=(
            jax.ShapeDtypeStruct((16, CHUNKS * CHUNK), jnp.bfloat16),
            jax.ShapeDtypeStruct((QUERY_ROWS, HEAD_SIZE), jnp.bfloat16),
            jax.ShapeDtypeStruct((POOL, PAGE_POSITIONS, HEAD_SIZE), jnp.bfloat16),
            jax.ShapeDtypeStruct((4, PAGE_POSITIONS, HEAD_SIZE), jnp.bfloat16),
        ),
        in_specs=[smem, smem, vmem, vmem, vmem, anywhere, vmem, vmem, vmem],
        out_specs=(vmem, vmem, vmem, vmem),
        scratch_shapes=[
            pltpu.VMEM(shape, jnp.float32 if shape == (128, 128) else jnp.bfloat16)
            for shape in scratch
        ]
        + [
            dma,
            dma((8,)),
            dma,
            dma,
            dma,
            dma,
            dma,
            dma,
            dma,
            dma,
            dma,
            dma((2, 4, 2)),
            dma,
            dma,
            dma,
            dma,
            dma((2,)),
            dma,
            dma,
            dma,
            dma((2, CHUNKS)),
            dma((2, 2)),
            dma((CHUNKS,)),
        ],
        compiler_params=pltpu.CompilerParams(
            collective_id=0, has_side_effects=True, vmem_limit_bytes=VMEM_LIMIT
        ),
        name="attention_layer",
    )(*operands)


CACHE_STEP = 8


def last_kernel(pages_in, turn_in, prefill_in, decode_in, cache, prefill_out, decode_out):
    me = lax.axis_index("pool")
    first = pl.program_id(0) * CACHE_STEP

    @pl.when(first == 0)
    def _():
        prefill_out[...] = prefill_in[...]
        for step in range(DECODE_STEPS):
            for head in range(HEADS_DEV):
                rows = decode_in[step * 32 + head * 8 : step * 32 + head * 8 + 8]
                decode_out[step, :, head * HEAD_SIZE : (head + 1) * HEAD_SIZE] = rows

    for k in range(CACHE_STEP):
        slot = (me - first - k + 2 * POOL) % POOL
        page = pages_in[slot]
        turn_page = turn_in[jnp.minimum(slot, 3)]
        turn_page = jnp.where(slot < 4, turn_page, jnp.zeros_like(turn_page))
        for kv in range(2):
            columns = slice(kv * 64, kv * 64 + 64)
            cache[0, k, 0, kv] = page[:, columns]
            cache[0, k, 1, kv] = turn_page[:, columns]


def last_call(pages_in, turn_in, prefill, decoded):
    vmem = pl.BlockSpec(memory_space=pltpu.VMEM)
    tail = (2, 2, PAGE_POSITIONS, 64)
    decode_shape = (DECODE_STEPS, 8, HEADS_DEV * HEAD_SIZE)
    return pl.pallas_call(
        last_kernel,
        grid=(POOL // CACHE_STEP,),
        out_shape=(
            jax.ShapeDtypeStruct((1, POOL) + tail, jnp.bfloat16),
            jax.ShapeDtypeStruct(prefill.shape, jnp.bfloat16),
            jax.ShapeDtypeStruct(decode_shape, jnp.bfloat16),
        ),
        in_specs=[vmem] * 4,
        out_specs=(
            pl.BlockSpec((1, CACHE_STEP) + tail, lambda i: (0, i, 0, 0, 0, 0)),
            pl.BlockSpec(prefill.shape, lambda i: (0, 0)),
            pl.BlockSpec(decode_shape, lambda i: (0, 0, 0)),
        ),
        compiler_params=pltpu.CompilerParams(vmem_limit_bytes=VMEM_LIMIT),
        name="lay_out_results",
    )(pages_in, turn_in, prefill, decoded)


def per_device(
    turn_query_rows,
    turn_key_value,
    prefix_page_store,
    prefix_pages,
    holder_table,
    out_weight,
    row_request,
    step_query,
    step_kv,
):
    rank = lax.axis_index("tp")
    fresh = lax.dynamic_slice_in_dim(step_kv, (rank // 2) * HEAD_SIZE, HEAD_SIZE, 3)
    fresh = jnp.transpose(fresh, (0, 2, 1, 3)).reshape(FRESH_ROWS, HEAD_SIZE)
    prefill_out, decode_rows, pages_in, turn_in = layer_call(
        prefix_pages,
        row_request,
        holder_table,
        prefix_page_store,
        turn_key_value.reshape(2, TURN_ROWS, KEY_VALUE_HEADS * HEAD_SIZE),
        out_weight,
        step_query,
        fresh,
        turn_query_rows.reshape(4, 2, 32, HEADS_DEV * HEAD_SIZE),
    )
    decode_cache, prefill_out, decode_out = last_call(
        pages_in, turn_in, prefill_out, decode_rows
    )
    return (prefill_out, decode_out, decode_cache)


def solution(mesh):
    placed = (
        P("pool", "tp"),
        P("pool", None, "tp", None),
        P("pool", None, "tp", None),
        P(),
        P(),
        P("tp", "pool"),
        P(),
        P(None, "pool", "tp"),
        P(None, "pool", None, None),
    )
    return jax.shard_map(
        per_device,
        mesh=mesh,
        in_specs=placed,
        out_specs=(
            P(("pool", "tp"), None),
            P(None, "pool", "tp"),
            P("pool", None, None, None, None, "tp"),
        ),
        check_vma=False,
    )
```
